512 devices in a mesh: dp: 128 (over y_hi, z, x), outer: 4 (over y_lo, core).
Axes of the slice: x: 4, y: 4 (y_hi: 2, y_lo: 2; y = y_hi * 2 + y_lo), z: 16, core: 2. Of those that a mesh axis runs over, the one named last changes fastest.
Arguments:
- image_embeds: bfloat16 [4, 32768, 1152], P('outer', 'dp'), may hold values from -6 to 6
- text_features: bfloat16 [4, 32768, 1152], P('outer', 'dp'), may hold values from -92 to 92
- projection: bfloat16 [1152, 1152], replicated, may hold values from -0.1875 to 0.1875
- pair_step: int32 [4, 32768], P('outer'), may hold values from 0 to 5
- pair_col: int32 [4, 32768], P('outer'), may hold values from 0 to 255
Outputs:
- grad_text: bfloat16 [4, 32768, 1152], P('outer', 'dp')
- grad_proj: float32 [1152, 1152], P('dp', 'outer')
The draws below stay inside these ranges and needn't reach their ends.
Inputs may be any that keep to these rules, and one draw needn't show every extreme that they name: pair_step of image row i in shard a points at text shard a - pair_step + 2 of the same group.
All inputs are finite; a program needn't handle non-finite values.
Results may differ from the reference program's by a relative error of at most 0.02.
Values may be sent and summed in bfloat16 or wider, within the bound.
No kernel may reach another device: no remote copies, remote signals or barrier semaphores. Data moves between devices by JAX's collectives and lax.ppermute only.
A program may use at most 64 MiB of HBM per device.

```python
import math
import jax
import jax.numpy as jnp
from jax import lax

D = 1152
E = 1152
B_DEV = 256
STEPS = 6
LEAD = 2
ROWS = 32768
N_DP = 128
N_OUTER = 4


def draw_text_features(key, part):
    key = jax.random.fold_in(key, 11)
    first_key, second_key = jax.random.split(key, 2)
    position = jnp.arange(D, dtype=jnp.float32) / D
    scales = 10.0 ** position * jnp.exp(jax.random.uniform(second_key, (D,), jnp.float32, -0.3, 0.3))
    values = jnp.clip(jax.random.normal(first_key, (N_OUTER, ROWS, D), jnp.float32), -6.0, 6.0) * scales
    return values.astype(jnp.bfloat16)


def plant(drawn, own_key, least, high):
    longest = drawn.shape.index(max(drawn.shape))
    spots = []
    for shift in (0, 1):
        where = [jax.random.randint(jax.random.fold_in(own_key, axis), (), 0, length) for axis, length in enumerate(drawn.shape)]
        where[longest] = (where[longest] + shift) % drawn.shape[longest]
        spots.append(tuple(where))
    return drawn.at[spots[0]].set(least).at[spots[1]].set(high)


def shard_levels(rng, dims, cuts, smallest, high):
    def one(axis_at, blocks):
        steps = jax.random.uniform(jax.random.fold_in(jax.random.fold_in(rng, 6), axis_at), (blocks,), jnp.float32, smallest / len(cuts), high / len(cuts))
        return jnp.repeat(jnp.exp(steps), dims[axis_at] // blocks).reshape((-1,) + (1,) * (len(dims) - axis_at - 1))

    level = one(*cuts[0])
    for cut in cuts[1:]:
        level = level * one(*cut)
    return level


def scatter_about(stream_key, shape, deviation, bound, shards=(), held_as=jnp.bfloat16):
    values = jax.random.normal(stream_key, shape, jnp.float32) * deviation
    if len(shards) > 0:
        values = shard_levels(stream_key, shape, shards, -0.22, 0.18) * values
    return jnp.clip(values, min=-bound, max=bound).astype(held_as)


def setup_inputs(seed: int = 0) -> dict:
    key_list = jax.random.split(jax.random.key(seed), 6)
    return {
        "image_embeds": scatter_about(key_list[0], (N_OUTER, ROWS, E), 1.0, 6.0, ((0, 4), (1, 128))),
        "text_features": draw_text_features(jax.random.fold_in(key_list[5], 71), 0),
        "projection": scatter_about(key_list[2], (D, E), D ** -0.5, 0.1875),
        "pair_step": plant(jax.random.randint(key_list[3], (N_OUTER, ROWS), 0, STEPS), jax.random.fold_in(key_list[3], 1), 0, STEPS - 1).astype(jnp.int32),
        "pair_col": plant(jax.random.randint(key_list[4], (N_OUTER, ROWS), 0, B_DEV), jax.random.fold_in(key_list[4], 1), 0, B_DEV - 1).astype(jnp.int32),
    }


LOGIT_SCALE = 10.0
LOGIT_BIAS = -3.0
LOSS_SCALE = 256.0
EPSILON = 1e-06

def unit_rows(values):
    values = values.astype(jnp.float32)
    inverse = lax.rsqrt(lax.optimization_barrier(jnp.sum(values * values, axis=-1, keepdims=True)) + EPSILON)
    return (values * inverse, inverse)

def reference(image_embeds, text_features, projection, pair_step, pair_col):
    stack_pos = jnp.repeat(jnp.arange(STEPS, dtype=jnp.int32), B_DEV)
    offsets = jnp.arange(STEPS, dtype=jnp.int32) - LEAD
    columns = lax.broadcasted_iota(jnp.int32, (STEPS * B_DEV, B_DEV), 1)
    grad_sum = jnp.zeros((D, E), jnp.float32)
    grads = []
    for group in range(N_OUTER):
        unit_img = unit_rows(image_embeds[group])[0].astype(jnp.bfloat16)
        features = text_features[group]
        hidden = jnp.dot(features, projection, preferred_element_type=jnp.float32)
        unit_text, inverse_norm = unit_rows(hidden)
        text_units = unit_text.astype(jnp.bfloat16)
        img_blocks = unit_img.reshape(N_DP, B_DEV, E)
        step_blocks = pair_step[group].reshape(N_DP, B_DEV)
        col_blocks = pair_col[group].reshape(N_DP, B_DEV)

        def one_shard(shard):
            shard_ids = (shard + offsets + N_DP) % N_DP
            images = img_blocks[shard_ids].reshape(STEPS * B_DEV, E)
            step_ids = step_blocks[shard_ids].reshape(STEPS * B_DEV)
            col_ids = col_blocks[shard_ids].reshape(STEPS * B_DEV)
            texts = lax.dynamic_slice_in_dim(text_units, (shard * B_DEV).astype(jnp.int32), B_DEV)
            logits = LOGIT_SCALE * jnp.dot(images, texts.T, preferred_element_type=jnp.float32) + LOGIT_BIAS
            positive = (step_ids == stack_pos)[:, None] & (col_ids[:, None] == columns)
            target = jnp.where(positive, 1.0, -1.0).astype(jnp.float32)
            weights = (-LOSS_SCALE * LOGIT_SCALE * target * jax.nn.sigmoid(-target * logits)).astype(jnp.bfloat16)
            return jnp.dot(weights.T, images, preferred_element_type=jnp.float32)
        unit_grad = lax.map(one_shard, jnp.arange(N_DP, dtype=jnp.int32)).reshape(ROWS, E)
        radial = lax.optimization_barrier(jnp.sum(unit_text * unit_grad, axis=-1, keepdims=True))
        hidden_grad = (inverse_norm * (unit_grad - unit_text * radial)).astype(jnp.bfloat16)
        grads.append(jnp.dot(hidden_grad, projection.T, preferred_element_type=jnp.float32).astype(jnp.bfloat16))

        def add_partial(carry, pieces):
            block_sum = jnp.dot(pieces[0].T, pieces[1], preferred_element_type=jnp.float32)
            rounded = lax.optimization_barrier(block_sum.astype(jnp.bfloat16)).astype(jnp.float32)
            return (carry + rounded, None)
        grad_sum, _ = lax.scan(add_partial, grad_sum, (features.reshape(N_DP, B_DEV, D), hidden_grad.reshape(N_DP, B_DEV, E)))
    grad_norm = jnp.sqrt(jnp.sum(grad_sum * grad_sum))
    factor = jnp.minimum(1.0, math.sqrt(D * E) / grad_norm)
    return (jnp.stack(grads), grad_sum * factor)
```

```python
import math

import jax
import jax.numpy as jnp
from jax import lax
from jax.sharding import Mesh, PartitionSpec as P

LOGIT_SCALE = 10.0
LOGIT_BIAS = -3.0
LOSS_SCALE = 256.0
EPSILON = 1e-06

SHARDS = 128
ROWS = 256
SHAPE = (2, 4, 4, 4, 2, 2)
AXES = ("yh", "zh", "zl", "x", "yl", "c")
DP = ("yh", "zh", "zl", "x")
OUTER = ("yl", "c")
Y = ("yl", "yh")
WIDTH = 2688
FIRST = 1280


def shifted(value, hop):
    pairs = [(source, (source + hop) % SHARDS) for source in range(SHARDS)]
    return lax.ppermute(value, DP, pairs)


def unit_rows(values):
    values = values.astype(jnp.float32)
    inverse = lax.rsqrt(jnp.sum(values * values, axis=-1, keepdims=True) + EPSILON)
    return (values * inverse, inverse)


def pair_grad(images, texts, step_ids, col_ids, position):
    logits = (
        LOGIT_SCALE * jnp.einsum("ke,ie->ki", texts, images, preferred_element_type=jnp.float32)
        + LOGIT_BIAS
    )
    rows = lax.broadcasted_iota(jnp.int32, logits.shape, 0)
    positive = (step_ids[None, :] == position) & (col_ids[None, :] == rows)
    target = jnp.where(positive, 1.0, -1.0).astype(jnp.float32)
    weights = (-LOSS_SCALE * LOGIT_SCALE * target * jax.nn.sigmoid(-target * logits)).astype(
        jnp.bfloat16
    )
    return jnp.einsum("ki,ie->ke", weights, images, preferred_element_type=jnp.float32)


def traded(value, axis):
    return lax.all_to_all(value, axis, split_axis=0, concat_axis=0)


def total(value):
    return jnp.sum(value.astype(jnp.float32), axis=0)


def local(image_embeds, text_features, projection, pair_step, pair_col):
    me = lax.axis_index(DP)
    core = lax.axis_index("c")
    image = image_embeds[0]
    before = shifted(image, 1)
    after = shifted(image, -1)
    before2 = shifted(before, 1)
    after2 = shifted(after, -1)
    after3 = shifted(before, -4)

    features = text_features[0]
    hidden = jnp.dot(features, projection, preferred_element_type=jnp.float32)
    unit_text, inverse_norm = unit_rows(hidden)
    text_units = unit_text.astype(jnp.bfloat16)
    step_table = pair_step.reshape(SHARDS, ROWS)
    col_table = pair_col.reshape(SHARDS, ROWS)
    unit_grad = None
    for position, block in ((2, image), (1, before), (3, after), (0, before2), (4, after2), (5, after3)):
        shard = (me + position - 2) % SHARDS
        steps = lax.dynamic_index_in_dim(step_table, shard, 0, keepdims=False)
        cols = lax.dynamic_index_in_dim(col_table, shard, 0, keepdims=False)
        images = unit_rows(block)[0].astype(jnp.bfloat16)
        part = pair_grad(images, text_units, steps, cols, position)
        unit_grad = part if unit_grad is None else unit_grad + part

    radial = jnp.sum(unit_text * unit_grad, axis=-1, keepdims=True)
    hidden_grad = (inverse_norm * (unit_grad - unit_text * radial)).astype(jnp.bfloat16)
    grad_text = jnp.einsum(
        "ke,de->kd", hidden_grad, projection, preferred_element_type=jnp.float32
    ).astype(jnp.bfloat16)

    ordered = features.reshape(ROWS, 2, 4, 4, 4, 9).transpose(5, 1, 4, 3, 2, 0)
    partial = jnp.einsum(
        "rpk,ke->rpe",
        ordered.reshape(9, SHARDS, ROWS),
        hidden_grad,
        preferred_element_type=jnp.float32,
    ).astype(jnp.bfloat16)
    partial = partial.reshape(9, SHARDS, 2, 2, 288).transpose(3, 2, 1, 0, 4)
    partial = partial.reshape(2, 2, SHARDS, 2592)
    partial = jnp.pad(partial, ((0, 0), (0, 0), (0, 0), (0, WIDTH - 2592)))
    there = lax.dynamic_index_in_dim(partial, 1 - core, 0, keepdims=False)
    here = lax.dynamic_index_in_dim(partial, core, 0, keepdims=False)
    came = lax.ppermute(there, "c", [(0, 1), (1, 0)])
    both = (here.astype(jnp.float32) + came.astype(jnp.float32)).astype(jnp.bfloat16)
    both = both.reshape(4, 4, 16, WIDTH)

    one = traded(both[..., :FIRST], Y)
    two = traded(both[..., FIRST:].transpose(1, 0, 2, 3), "x")
    one = traded(total(one).astype(jnp.bfloat16), "x")
    two = traded(total(two).astype(jnp.bfloat16), Y)
    rows = jnp.concatenate([total(one), total(two)], axis=-1).astype(jnp.bfloat16)
    rows = total(traded(rows.reshape(4, 4, WIDTH), "zl")).astype(jnp.bfloat16)
    rows = total(traded(jnp.broadcast_to(rows[None], (4, 4, WIDTH)), "zh"))
    square = jnp.sum(rows * rows)
    for axis in ("c", Y, "x", "zl"):
        square = lax.psum(square, axis)
    owned = lax.dynamic_index_in_dim(rows, lax.axis_index("zh"), 0, keepdims=False)
    owned = owned[:2592].reshape(9, 288)
    threshold = math.sqrt(projection.shape[0] * projection.shape[1])
    factor = jnp.minimum(1.0, threshold / jnp.sqrt(square))
    return (grad_text[None], owned * factor)


def solution(mesh):
    split = Mesh(mesh.devices.reshape(SHAPE), AXES)
    placed = (
        P(OUTER, DP, None),
        P(OUTER, DP, None),
        P(),
        P(OUTER, None),
        P(OUTER, None),
    )
    return jax.shard_map(
        local,
        mesh=split,
        in_specs=placed,
        out_specs=(P(OUTER, DP, None), P(DP, OUTER)),
        check_vma=False,
    )
```

```python
import functools
import math

import jax
import jax.numpy as jnp
from jax import lax
from jax.experimental import pallas as pl
from jax.experimental.pallas import tpu as pltpu
from jax.sharding import Mesh, PartitionSpec as P

LOGIT_SCALE = 10.0
LOGIT_BIAS = -3.0
LOSS_SCALE = 256.0
EPSILON = 1e-06

SHARDS = 128
ROWS = 256
D = 1152
E = 1152
SHAPE = (2, 4, 4, 4, 2, 2)
AXES = ("yh", "zh", "zl", "x", "yl", "c")
DP = ("yh", "zh", "zl", "x")
OUTER = ("yl", "c")
PLANE = ("yl", "yh", "x")
RB = 9
CB = 288
MAIN = 256
REST = 32
SPLIT = RB * MAIN
WIDTH = 2688
PICK = 2 * MAIN + 2 * 128

F32 = jnp.float32
BF16 = jnp.bfloat16
VMEM = pl.BlockSpec(memory_space=pltpu.VMEM)
SMEM = pl.BlockSpec(memory_space=pltpu.SMEM)


def shifted(value, hop):
    pairs = [(source, (source + hop) % SHARDS) for source in range(SHARDS)]
    return lax.ppermute(value, DP, pairs)


def dot(a, b):
    return jnp.dot(a, b, preferred_element_type=F32)


def dot_t(a, b):
    return lax.dot_general(a, b, (((1,), (1,)), ((), ())), preferred_element_type=F32)


def unit_rows(values):
    values = values.astype(F32)
    inverse = lax.rsqrt(jnp.sum(values * values, axis=-1, keepdims=True) + EPSILON)
    return values * inverse, inverse


def pair_grad(place, step_ref, col_ref, texts, block, position):
    images = unit_rows(block)[0].astype(BF16)
    shard = (place + (SHARDS + position - 2)) % SHARDS
    spot = pl.ds(pl.multiple_of(shard * ROWS, ROWS), ROWS)
    steps = step_ref[:, spot]
    cols = col_ref[:, spot]
    logits = LOGIT_SCALE * dot_t(texts, images) + LOGIT_BIAS
    rows = lax.broadcasted_iota(jnp.int32, logits.shape, 0)
    positive = (steps == position) & (cols == rows)
    scale = LOSS_SCALE * LOGIT_SCALE
    chance = 1.0 / (1.0 + jnp.exp(jnp.where(positive, logits, -logits)))
    weights = (jnp.where(positive, -scale, scale) * chance).astype(BF16)
    return dot(weights, images)


def first_kernel(place_ref, feat_ref, proj_ref, image_ref, step_ref, col_ref, unit_ref, inv_ref, text_ref, acc_ref):
    hidden = dot(feat_ref[...], proj_ref[...])
    unit, inverse = unit_rows(hidden)
    texts = unit.astype(BF16)
    unit_ref[...] = unit
    inv_ref[...] = jnp.broadcast_to(inverse, inv_ref.shape)
    text_ref[...] = texts
    acc_ref[...] = pair_grad(place_ref[0], step_ref, col_ref, texts, image_ref[...], 2)


def column_of(lane, core):
    tail = lane - 2 * MAIN
    pair = jnp.where(lane < 2 * MAIN, lane >> 8, tail >> 7)
    inside = jnp.where(lane < 2 * MAIN, lane & (MAIN - 1), MAIN + (lane & (REST - 1)))
    return CB * (2 * pair + core) + inside


def second_kernel(
    place_ref, feat_ref, before_ref, after_ref, step_ref, col_ref, text_ref, acc_ref, out_ref, turned_ref, there_ref, here_ref
):
    texts = text_ref[...]
    place = place_ref[0]
    total = acc_ref[...] + pair_grad(place, step_ref, col_ref, texts, before_ref[...], 1)
    out_ref[...] = total + pair_grad(place, step_ref, col_ref, texts, after_ref[...], 3)

    spot = lax.broadcasted_iota(jnp.int32, (D, 1), 0)
    within, peer = spot >> 7, spot & (SHARDS - 1)
    yh, x, zl, zh = peer >> 6, (peer >> 4) & 3, (peer >> 2) & 3, peer & 3
    source = RB * (64 * yh + 16 * zh + 4 * zl + x) + within
    lanes = lax.broadcasted_iota(jnp.int32, (D, D), 1)
    order = jnp.where(lanes == source, 1.0, 0.0).astype(BF16)
    turned_ref[...] = dot_t(order, feat_ref[...]).astype(BF16)

    core = place_ref[1]
    lane = lax.broadcasted_iota(jnp.int32, (1, PICK), 1)
    rows = lax.broadcasted_iota(jnp.int32, (E, PICK), 0)
    there_ref[...] = jnp.where(rows == column_of(lane, 1 - core), 1.0, 0.0).astype(BF16)
    here_ref[...] = jnp.where(rows == column_of(lane, core), 1.0, 0.0).astype(BF16)


def write_partial(turned_ref, picked, out_ref):
    group = lax.broadcasted_iota(jnp.int32, (SHARDS, 128), 1) // REST
    rest = [[jnp.zeros((SHARDS, 128), F32) for _ in range(3)] for _ in range(2)]
    for r in range(RB):
        block = dot(turned_ref[r * SHARDS : (r + 1) * SHARDS, :], picked)
        for pair in range(2):
            out_ref[pair, :, r * MAIN : (r + 1) * MAIN] = block[:, pair * MAIN : (pair + 1) * MAIN].astype(BF16)
            tail = block[:, 2 * MAIN + pair * 128 : 2 * MAIN + (pair + 1) * 128]
            rest[pair][r // 4] = jnp.where(group == r % 4, tail, rest[pair][r // 4])
    for pair in range(2):
        for t in range(3):
            out_ref[pair, :, SPLIT + t * 128 : SPLIT + (t + 1) * 128] = rest[pair][t].astype(BF16)


def third_kernel(
    place_ref, before2_ref, after2_ref, after3_ref, step_ref, col_ref, text_ref, acc_ref, unit_ref, inv_ref, turned_ref, pick_ref,
    grad_ref, out_ref,
):
    texts = text_ref[...]
    place = place_ref[0]
    total = acc_ref[...]
    for position, block in ((0, before2_ref), (4, after2_ref), (5, after3_ref)):
        total = total + pair_grad(place, step_ref, col_ref, texts, block[...], position)
    unit = unit_ref[...]
    radial = jnp.sum(unit * total, axis=-1, keepdims=True)
    grad = (inv_ref[:, :1] * (total - unit * radial)).astype(BF16)
    grad_ref[...] = grad
    write_partial(turned_ref, dot(grad, pick_ref[...]).astype(BF16), out_ref)


def fourth_kernel(grad_ref, turned_ref, pick_ref, proj_ref, out_ref, text_grad_ref):
    grad = grad_ref[...]
    write_partial(turned_ref, dot(grad, pick_ref[...]).astype(BF16), out_ref)
    text_grad_ref[...] = dot_t(grad, proj_ref[...]).astype(BF16)


def block_kernel(place_ref, came_ref, block_ref, square_ref):
    rows = jnp.sum(came_ref[...].astype(F32), axis=0)
    sums = jnp.sum(rows * rows, axis=0, keepdims=True)
    square = functools.reduce(jnp.add, [sums[:, t * 128 : (t + 1) * 128] for t in range(WIDTH // 128)])
    lines = lax.broadcasted_iota(jnp.int32, (8, 128), 0)
    square = jnp.where(lines == 0, jnp.broadcast_to(square, (8, 128)), 0.0)
    square_ref[...] = jnp.broadcast_to(square[None], square_ref.shape)
    mine = lax.broadcasted_iota(jnp.int32, rows.shape, 0) == place_ref[2]
    own = jnp.sum(jnp.where(mine, rows, 0.0), axis=0, keepdims=True)
    for r in range(RB):
        block_ref[r : r + 1, :MAIN] = own[:, r * MAIN : (r + 1) * MAIN]
        block_ref[r : r + 1, MAIN:] = own[:, SPLIT + r * REST : SPLIT + (r + 1) * REST]


def clip_kernel(square_ref, block_ref, out_ref):
    square = jnp.sum(jnp.sum(square_ref[...], axis=0), keepdims=True)
    factor = jnp.minimum(1.0, math.sqrt(D * E) * lax.rsqrt(square))
    out_ref[...] = block_ref[...] * factor


def call(kernel, inputs, outputs, flops, size, name):
    return pl.pallas_call(
        kernel,
        out_shape=[jax.ShapeDtypeStruct(shape, dtype) for shape, dtype in outputs],
        in_specs=[SMEM if value.shape == (3,) else VMEM for value in inputs],
        out_specs=[VMEM] * len(outputs),
        compiler_params=pltpu.CompilerParams(vmem_limit_bytes=size << 20),
        cost_estimate=pl.CostEstimate(flops=flops, bytes_accessed=4 << 20, transcendentals=0),
        name=name,
    )(*inputs)


def traded(value, axis):
    return lax.all_to_all(value, axis, split_axis=0, concat_axis=0)


def total(value):
    return jnp.sum(value.astype(F32), axis=0)


def local(image_embeds, text_features, projection, pair_step, pair_col):
    place = jnp.stack([lax.axis_index(DP), lax.axis_index("c"), lax.axis_index("zh")]).astype(jnp.int32)
    image = image_embeds[0]
    features = text_features[0]
    before = shifted(image, 1)
    after = shifted(image, -1)
    before2 = shifted(before, 1)
    after2 = shifted(after, -1)
    after3 = shifted(before, -4)

    full = (ROWS, E)
    unit, inverse, texts, acc = call(
        first_kernel,
        (place, features, projection, image, pair_step, pair_col),
        ((full, F32), ((ROWS, 128), F32), (full, BF16), (full, F32)),
        1 << 30, 24, "hidden_and_own",
    )
    acc, turned, pick_there, pick_here = call(
        second_kernel,
        (place, features, before, after, pair_step, pair_col, texts, acc),
        ((full, F32), ((D, ROWS), BF16), ((E, PICK), BF16), ((E, PICK), BF16)),
        1 << 30, 32, "near_pairs",
    )
    shape = (2, SHARDS, WIDTH)
    grad, there = call(
        third_kernel,
        (place, before2, after2, after3, pair_step, pair_col, texts, acc, unit, inverse, turned, pick_there),
        ((full, BF16), (shape, BF16)),
        1 << 30, 32, "far_pairs",
    )
    came = lax.ppermute(there, "c", [(0, 1), (1, 0)])
    here, grad_text = call(
        fourth_kernel, (grad, turned, pick_here, projection), ((shape, BF16), (full, BF16)), 1 << 30, 32, "own_half"
    )
    both = (here.astype(F32) + came.astype(F32)).astype(BF16)

    rows = total(traded(both.reshape(16, 16, WIDTH), PLANE)).astype(BF16)
    rows = total(traded(rows.reshape(4, 4, WIDTH), "zl")).astype(BF16)
    rows = traded(jnp.broadcast_to(rows[None], (4, 4, WIDTH)), "zh")
    block, square = call(
        block_kernel, (place, rows), (((RB, CB), F32), ((8, 8, 128), F32)), 1 << 20, 16, "block"
    )
    square = total(traded(square, ("yl", "yh", "c")))
    square = traded(jnp.broadcast_to(square[None], (16, 8, 128)), ("x", "zl"))
    (block,) = call(clip_kernel, (square, block), (((RB, CB), F32),), 1 << 20, 16, "clip")
    return (grad_text[None], block)


def solution(mesh):
    split = Mesh(mesh.devices.reshape(SHAPE), AXES)
    placed = (
        P(OUTER, DP, None),
        P(OUTER, DP, None),
        P(),
        P(OUTER, None),
        P(OUTER, None),
    )
    return jax.shard_map(
        local,
        mesh=split,
        in_specs=placed,
        out_specs=(P(OUTER, DP, None), P(DP, OUTER)),
        check_vma=False,
    )
```

```python
import functools
import math

import jax
import jax.numpy as jnp
from jax import lax
from jax.experimental import pallas as pl
from jax.experimental.pallas import tpu as pltpu
from jax.sharding import Mesh, PartitionSpec as P

LOGIT_SCALE = 10.0
LOGIT_BIAS = -3.0
LOSS_SCALE = 256.0
EPSILON = 1e-06

SHARDS = 128
ROWS = 256
D = 1152
E = 1152
SHAPE = (2, 4, 4, 4, 2, 2)
AXES = ("yh", "zh", "zl", "x", "yl", "c")
DP = ("yh", "zh", "zl", "x")
OUTER = ("yl", "c")
PLANE = ("yh", "yl", "x")
LINE = ("zh", "zl")
RB = 9
CB = 288
MAIN = 256
REST = 32
SPLIT = RB * MAIN
WIDTH = 2688
PICK = 2 * MAIN + 2 * 128

F32 = jnp.float32
BF16 = jnp.bfloat16
VMEM = pl.BlockSpec(memory_space=pltpu.VMEM)
SMEM = pl.BlockSpec(memory_space=pltpu.SMEM)


RIGHT = (1, 1, 1, -3)
LEFT = (-1, -1, -1, -1)
RIGHT2 = (1, 1, 1, 1)
LEFT2 = (-1, -1, 3, -1)
ACROSS = (4, -4, -4, -4)
RIGHT_AT = (5, 1, 1, 1)
LEFT_AT = (3, 3, 3, 3)
RIGHT2_AT = (0, 4, 0, 0)
LEFT2_AT = (4, 0, 4, 4)
ACROSS_AT = (1, 5, 5, 5)


def shifted(value, hops):
    pairs = [(source, (source + hops[source % 4]) % SHARDS) for source in range(SHARDS)]
    return lax.ppermute(value, DP, pairs)


def position_of(x, places):
    return jnp.where(x == 0, places[0], jnp.where(x == 1, places[1], jnp.where(x == 2, places[2], places[3])))


def dot(a, b):
    return jnp.dot(a, b, preferred_element_type=F32)


def dot_t(a, b):
    return lax.dot_general(a, b, (((1,), (1,)), ((), ())), preferred_element_type=F32)


def unit_rows(values):
    values = values.astype(F32)
    inverse = lax.rsqrt(jnp.sum(values * values, axis=-1, keepdims=True) + EPSILON)
    return values * inverse, inverse


def pair_grad(place, step_ref, col_ref, texts, block, position):
    images = unit_rows(block)[0].astype(BF16)
    shard = (place + (position + (SHARDS - 2))) & (SHARDS - 1)
    spot = pl.ds(pl.multiple_of(shard * ROWS, ROWS), ROWS)
    steps = step_ref[:, spot]
    cols = col_ref[:, spot]
    logits = LOGIT_SCALE * dot_t(texts, images) + LOGIT_BIAS
    rows = lax.broadcasted_iota(jnp.int32, logits.shape, 0)
    positive = (steps == position) & (cols == rows)
    scale = LOSS_SCALE * LOGIT_SCALE
    chance = 1.0 / (1.0 + jnp.exp(jnp.where(positive, logits, -logits)))
    weights = (jnp.where(positive, -scale, scale) * chance).astype(BF16)
    return dot(weights, images)


def first_kernel(place_ref, feat_ref, proj_ref, image_ref, step_ref, col_ref, unit_ref, inv_ref, text_ref, acc_ref):
    hidden = dot(feat_ref[...], proj_ref[...])
    unit, inverse = unit_rows(hidden)
    texts = unit.astype(BF16)
    unit_ref[...] = unit
    inv_ref[...] = jnp.broadcast_to(inverse, inv_ref.shape)
    text_ref[...] = texts
    acc_ref[...] = pair_grad(place_ref[0], step_ref, col_ref, texts, image_ref[...], 2)


def column_of(lane, core):
    tail = lane - 2 * MAIN
    pair = jnp.where(lane < 2 * MAIN, lane >> 8, tail >> 7)
    inside = jnp.where(lane < 2 * MAIN, lane & (MAIN - 1), MAIN + (lane & (REST - 1)))
    return CB * (2 * pair + core) + inside


def second_kernel(
    place_ref, feat_ref, before_ref, after_ref, step_ref, col_ref, text_ref, acc_ref, out_ref, turned_ref, there_ref, here_ref
):
    texts = text_ref[...]
    place = place_ref[0]
    total = acc_ref[...] + pair_grad(place, step_ref, col_ref, texts, before_ref[...], place_ref[2])
    out_ref[...] = total + pair_grad(place, step_ref, col_ref, texts, after_ref[...], 3)

    spot = lax.broadcasted_iota(jnp.int32, (D, 1), 0)
    within, peer = spot >> 7, spot & (SHARDS - 1)
    yh, x, z = peer >> 6, (peer >> 4) & 3, peer & 15
    source = RB * (64 * yh + 4 * z + x) + within
    lanes = lax.broadcasted_iota(jnp.int32, (D, D), 1)
    order = jnp.where(lanes == source, 1.0, 0.0).astype(BF16)
    turned_ref[...] = dot_t(order, feat_ref[...]).astype(BF16)

    core = place_ref[1]
    lane = lax.broadcasted_iota(jnp.int32, (1, PICK), 1)
    rows = lax.broadcasted_iota(jnp.int32, (E, PICK), 0)
    there_ref[...] = jnp.where(rows == column_of(lane, 1 - core), 1.0, 0.0).astype(BF16)
    here_ref[...] = jnp.where(rows == column_of(lane, core), 1.0, 0.0).astype(BF16)


def write_partial(turned_ref, picked, out_ref):
    half = SHARDS // 2
    group = lax.broadcasted_iota(jnp.int32, (SHARDS, 128), 1) // REST
    rest = [[jnp.zeros((SHARDS, 128), F32) for _ in range(3)] for _ in range(2)]
    for r in range(RB):
        block = dot(turned_ref[r * SHARDS : (r + 1) * SHARDS, :], picked)
        for pair in range(2):
            main = block[:, pair * MAIN : (pair + 1) * MAIN].astype(BF16)
            for yh in range(2):
                out_ref[yh, pair, :, r * MAIN : (r + 1) * MAIN] = main[yh * half : (yh + 1) * half]
            tail = block[:, 2 * MAIN + pair * 128 : 2 * MAIN + (pair + 1) * 128]
            rest[pair][r // 4] = jnp.where(group == r % 4, tail, rest[pair][r // 4])
    for pair in range(2):
        for t in range(3):
            tail = rest[pair][t].astype(BF16)
            for yh in range(2):
                out_ref[yh, pair, :, SPLIT + t * 128 : SPLIT + (t + 1) * 128] = tail[yh * half : (yh + 1) * half]


def third_kernel(
    place_ref, right_ref, left_ref, across_ref, step_ref, col_ref, text_ref, acc_ref, unit_ref, inv_ref, turned_ref, pick_ref,
    grad_ref, out_ref,
):
    texts = text_ref[...]
    place = place_ref[0]
    total = acc_ref[...]
    for at, block in ((3, right_ref), (4, left_ref), (5, across_ref)):
        total = total + pair_grad(place, step_ref, col_ref, texts, block[...], place_ref[at])
    unit = unit_ref[...]
    radial = jnp.sum(unit * total, axis=-1, keepdims=True)
    grad = (inv_ref[:, :1] * (total - unit * radial)).astype(BF16)
    grad_ref[...] = grad
    write_partial(turned_ref, dot(grad, pick_ref[...]).astype(BF16), out_ref)


def fourth_kernel(grad_ref, turned_ref, pick_ref, proj_ref, out_ref, text_grad_ref):
    grad = grad_ref[...]
    write_partial(turned_ref, dot(grad, pick_ref[...]).astype(BF16), out_ref)
    text_grad_ref[...] = dot_t(grad, proj_ref[...]).astype(BF16)


def block_kernel(came_ref, block_ref, square_ref):
    own = jnp.sum(came_ref[...].astype(F32), axis=0, keepdims=True)
    sums = own * own
    square = functools.reduce(jnp.add, [sums[:, t * 128 : (t + 1) * 128] for t in range(WIDTH // 128)])
    lines = lax.broadcasted_iota(jnp.int32, (8, 128), 0)
    square = jnp.where(lines == 0, jnp.broadcast_to(square, (8, 128)), 0.0)
    square_ref[...] = jnp.broadcast_to(square[None], square_ref.shape)
    for r in range(RB):
        block_ref[r : r + 1, :MAIN] = own[:, r * MAIN : (r + 1) * MAIN]
        block_ref[r : r + 1, MAIN:] = own[:, SPLIT + r * REST : SPLIT + (r + 1) * REST]


def clip_kernel(square_ref, block_ref, out_ref):
    square = jnp.sum(jnp.sum(square_ref[...], axis=0), keepdims=True)
    factor = jnp.minimum(1.0, math.sqrt(D * E) * lax.rsqrt(square))
    out_ref[...] = block_ref[...] * factor


def call(kernel, inputs, outputs, flops, size, name):
    return pl.pallas_call(
        kernel,
        out_shape=[jax.ShapeDtypeStruct(shape, dtype) for shape, dtype in outputs],
        in_specs=[SMEM if value.ndim == 1 else VMEM for value in inputs],
        out_specs=[VMEM] * len(outputs),
        compiler_params=pltpu.CompilerParams(vmem_limit_bytes=size << 20),
        cost_estimate=pl.CostEstimate(flops=flops, bytes_accessed=4 << 20, transcendentals=0),
        name=name,
    )(*inputs)


def traded(value, axis):
    return lax.all_to_all(value, axis, split_axis=0, concat_axis=0)


def total(value):
    return jnp.sum(value.astype(F32), axis=0)


def local(image_embeds, text_features, projection, pair_step, pair_col):
    x = lax.axis_index("x")
    places = (RIGHT_AT, RIGHT2_AT, LEFT2_AT, ACROSS_AT)
    place = jnp.stack([lax.axis_index(DP), lax.axis_index("c")] + [position_of(x, at) for at in places]).astype(jnp.int32)
    image = image_embeds[0]
    features = text_features[0]
    right = shifted(image, RIGHT)
    left = shifted(image, LEFT)
    right2 = shifted(right, RIGHT2)
    left2 = shifted(left, LEFT2)
    across = shifted(right, ACROSS)

    full = (ROWS, E)
    unit, inverse, texts, acc = call(
        first_kernel,
        (place, features, projection, image, pair_step, pair_col),
        ((full, F32), ((ROWS, 128), F32), (full, BF16), (full, F32)),
        1 << 30, 24, "hidden_and_own",
    )
    acc, turned, pick_there, pick_here = call(
        second_kernel,
        (place, features, right, left, pair_step, pair_col, texts, acc),
        ((full, F32), ((D, ROWS), BF16), ((E, PICK), BF16), ((E, PICK), BF16)),
        1 << 30, 32, "near_pairs",
    )
    shape = (2, 2, SHARDS // 2, WIDTH)
    grad, there = call(
        third_kernel,
        (place, right2, left2, across, pair_step, pair_col, texts, acc, unit, inverse, turned, pick_there),
        ((full, BF16), (shape, BF16)),
        1 << 30, 32, "far_pairs",
    )
    came = lax.ppermute(there, "c", [(0, 1), (1, 0)])
    here, grad_text = call(
        fourth_kernel, (grad, turned, pick_here, projection), ((shape, BF16), (full, BF16)), 1 << 30, 32, "own_half"
    )
    both = (here.astype(F32) + came.astype(F32)).astype(BF16)

    rows = total(traded(both.reshape(16, 16, WIDTH), PLANE)).astype(BF16)
    rows = traded(rows.reshape(16, 1, WIDTH), LINE).reshape(16, WIDTH)
    block, square = call(block_kernel, (rows,), (((RB, CB), F32), ((32, 8, 128), F32)), 1 << 20, 16, "block")
    square = total(traded(square, PLANE + ("c",)))
    square = traded(jnp.broadcast_to(square[None], (16, 8, 128)), LINE)
    (block,) = call(clip_kernel, (square, block), (((RB, CB), F32),), 1 << 20, 16, "clip")
    return (grad_text[None], block)


def solution(mesh):
    split = Mesh(mesh.devices.reshape(SHAPE), AXES)
    placed = (
        P(OUTER, DP, None),
        P(OUTER, DP, None),
        P(),
        P(OUTER, None),
        P(OUTER, None),
    )
    return jax.shard_map(
        local,
        mesh=split,
        in_specs=placed,
        out_specs=(P(OUTER, DP, None), P(DP, OUTER)),
        check_vma=False,
    )
```

```python
import functools
import math

import jax
import jax.numpy as jnp
from jax import lax
from jax.experimental import pallas as pl
from jax.experimental.pallas import tpu as pltpu
from jax.sharding import Mesh, PartitionSpec as P

LOGIT_SCALE = 10.0
LOGIT_BIAS = -3.0
LOSS_SCALE = 256.0
EPSILON = 1e-06

SHARDS = 128
ROWS = 256
D = 1152
E = 1152
SHAPE = (2, 4, 2, 2, 4, 2, 2)
AXES = ("yh", "zh", "z1", "z0", "x", "yl", "c")
DP = ("yh", "zh", "z1", "z0", "x")
OUTER = ("yl", "c")
NEAR = ("yh", "yl", "x", "z0")
RB = 9
CB = 288
MAIN = 256
REST = 32
SPLIT = RB * MAIN
WIDTH = 2688
PICK = 2 * MAIN + 2 * 128

F32 = jnp.float32
BF16 = jnp.bfloat16
VMEM = pl.BlockSpec(memory_space=pltpu.VMEM)
SMEM = pl.BlockSpec(memory_space=pltpu.SMEM)


RIGHT = (1, 1, 1, -3)
LEFT = (-1, -1, -1, -1)
RIGHT2 = (1, 1, 1, 1)
LEFT2 = (-1, -1, 3, -1)
ACROSS = (4, -4, -4, -4)
RIGHT_AT = (5, 1, 1, 1)
LEFT_AT = (3, 3, 3, 3)
RIGHT2_AT = (0, 4, 0, 0)
LEFT2_AT = (4, 0, 4, 4)
ACROSS_AT = (1, 5, 5, 5)


def shifted(value, hops):
    pairs = [(source, (source + hops[source % 4]) % SHARDS) for source in range(SHARDS)]
    return lax.ppermute(value, DP, pairs)


def position_of(x, places):
    return jnp.where(x == 0, places[0], jnp.where(x == 1, places[1], jnp.where(x == 2, places[2], places[3])))


def dot(a, b):
    return jnp.dot(a, b, preferred_element_type=F32)


def dot_t(a, b):
    return lax.dot_general(a, b, (((1,), (1,)), ((), ())), preferred_element_type=F32)


def unit_rows(values):
    values = values.astype(F32)
    inverse = lax.rsqrt(jnp.sum(values * values, axis=-1, keepdims=True) + EPSILON)
    return values * inverse, inverse


def pair_grad(place, step_ref, col_ref, texts, block, position):
    images = unit_rows(block)[0].astype(BF16)
    shard = (place + (position + (SHARDS - 2))) & (SHARDS - 1)
    spot = pl.ds(pl.multiple_of(shard * ROWS, ROWS), ROWS)
    steps = step_ref[:, spot]
    cols = col_ref[:, spot]
    logits = LOGIT_SCALE * dot_t(texts, images) + LOGIT_BIAS
    rows = lax.broadcasted_iota(jnp.int32, logits.shape, 0)
    positive = (steps == position) & (cols == rows)
    scale = LOSS_SCALE * LOGIT_SCALE
    chance = 1.0 / (1.0 + jnp.exp(jnp.where(positive, logits, -logits)))
    weights = (jnp.where(positive, -scale, scale) * chance).astype(BF16)
    return dot(weights, images)


def first_kernel(place_ref, feat_ref, proj_ref, image_ref, step_ref, col_ref, unit_ref, inv_ref, text_ref, acc_ref):
    hidden = dot(feat_ref[...], proj_ref[...])
    unit, inverse = unit_rows(hidden)
    texts = unit.astype(BF16)
    unit_ref[...] = unit
    inv_ref[...] = jnp.broadcast_to(inverse, inv_ref.shape)
    text_ref[...] = texts
    acc_ref[...] = pair_grad(place_ref[0], step_ref, col_ref, texts, image_ref[...], 2)


def column_of(lane, core):
    tail = lane - 2 * MAIN
    pair = jnp.where(lane < 2 * MAIN, lane >> 8, tail >> 7)
    inside = jnp.where(lane < 2 * MAIN, lane & (MAIN - 1), MAIN + (lane & (REST - 1)))
    return CB * (2 * pair + core) + inside


def second_kernel(
    place_ref, feat_ref, before_ref, after_ref, step_ref, col_ref, text_ref, acc_ref, out_ref, turned_ref, there_ref, here_ref
):
    texts = text_ref[...]
    place = place_ref[0]
    total = acc_ref[...] + pair_grad(place, step_ref, col_ref, texts, before_ref[...], place_ref[2])
    out_ref[...] = total + pair_grad(place, step_ref, col_ref, texts, after_ref[...], 3)

    spot = lax.broadcasted_iota(jnp.int32, (D, 1), 0)
    within, peer = spot >> 7, spot & (SHARDS - 1)
    yh, x, z0, z = peer >> 6, (peer >> 4) & 3, (peer >> 3) & 1, peer & 7
    source = RB * (64 * yh + 8 * z + 4 * z0 + x) + within
    lanes = lax.broadcasted_iota(jnp.int32, (D, D), 1)
    order = jnp.where(lanes == source, 1.0, 0.0).astype(BF16)
    turned_ref[...] = dot_t(order, feat_ref[...]).astype(BF16)

    core = place_ref[1]
    lane = lax.broadcasted_iota(jnp.int32, (1, PICK), 1)
    rows = lax.broadcasted_iota(jnp.int32, (E, PICK), 0)
    there_ref[...] = jnp.where(rows == column_of(lane, 1 - core), 1.0, 0.0).astype(BF16)
    here_ref[...] = jnp.where(rows == column_of(lane, core), 1.0, 0.0).astype(BF16)


def write_partial(turned_ref, picked, out_ref):
    half = SHARDS // 2
    group = lax.broadcasted_iota(jnp.int32, (SHARDS, 128), 1) // REST
    rest = [[jnp.zeros((SHARDS, 128), F32) for _ in range(3)] for _ in range(2)]
    for r in range(RB):
        block = dot(turned_ref[r * SHARDS : (r + 1) * SHARDS, :], picked)
        for pair in range(2):
            main = block[:, pair * MAIN : (pair + 1) * MAIN].astype(BF16)
            for yh in range(2):
                out_ref[yh, pair, :, r * MAIN : (r + 1) * MAIN] = main[yh * half : (yh + 1) * half]
            tail = block[:, 2 * MAIN + pair * 128 : 2 * MAIN + (pair + 1) * 128]
            rest[pair][r // 4] = jnp.where(group == r % 4, tail, rest[pair][r // 4])
    for pair in range(2):
        for t in range(3):
            tail = rest[pair][t].astype(BF16)
            for yh in range(2):
                out_ref[yh, pair, :, SPLIT + t * 128 : SPLIT + (t + 1) * 128] = tail[yh * half : (yh + 1) * half]


def far_kernel(at, place_ref, image_ref, step_ref, col_ref, text_ref, acc_ref, out_ref):
    part = pair_grad(place_ref[0], step_ref, col_ref, text_ref[...], image_ref[...], place_ref[at])
    out_ref[...] = acc_ref[...] + part


def third_kernel(
    place_ref, left_ref, step_ref, col_ref, text_ref, acc_ref, unit_ref, inv_ref, turned_ref, pick_ref, grad_ref, out_ref
):
    part = pair_grad(place_ref[0], step_ref, col_ref, text_ref[...], left_ref[...], place_ref[4])
    total = acc_ref[...] + part
    unit = unit_ref[...]
    radial = jnp.sum(unit * total, axis=-1, keepdims=True)
    grad = (inv_ref[:, :1] * (total - unit * radial)).astype(BF16)
    grad_ref[...] = grad
    write_partial(turned_ref, dot(grad, pick_ref[...]).astype(BF16), out_ref)


def fourth_kernel(grad_ref, turned_ref, pick_ref, proj_ref, out_ref, text_grad_ref):
    grad = grad_ref[...]
    write_partial(turned_ref, dot(grad, pick_ref[...]).astype(BF16), out_ref)
    text_grad_ref[...] = dot_t(grad, proj_ref[...]).astype(BF16)


def block_kernel(place_ref, came_ref, block_ref, square_ref):
    rows = jnp.sum(came_ref[...].astype(F32), axis=0)
    sums = jnp.sum(rows * rows, axis=0, keepdims=True)
    square = functools.reduce(jnp.add, [sums[:, t * 128 : (t + 1) * 128] for t in range(WIDTH // 128)])
    lines = lax.broadcasted_iota(jnp.int32, (8, 128), 0)
    square = jnp.where(lines == 0, jnp.broadcast_to(square, (8, 128)), 0.0)
    square_ref[...] = jnp.broadcast_to(square[None], square_ref.shape)
    mine = lax.broadcasted_iota(jnp.int32, rows.shape, 0) == place_ref[6]
    own = jnp.sum(jnp.where(mine, rows, 0.0), axis=0, keepdims=True)
    for r in range(RB):
        block_ref[r : r + 1, :MAIN] = own[:, r * MAIN : (r + 1) * MAIN]
        block_ref[r : r + 1, MAIN:] = own[:, SPLIT + r * REST : SPLIT + (r + 1) * REST]


def clip_kernel(square_ref, block_ref, out_ref):
    square = jnp.sum(jnp.sum(square_ref[...], axis=0), keepdims=True)
    factor = jnp.minimum(1.0, math.sqrt(D * E) * lax.rsqrt(square))
    out_ref[...] = block_ref[...] * factor


def call(kernel, inputs, outputs, flops, size, name):
    return pl.pallas_call(
        kernel,
        out_shape=[jax.ShapeDtypeStruct(shape, dtype) for shape, dtype in outputs],
        in_specs=[SMEM if value.ndim == 1 else VMEM for value in inputs],
        out_specs=[VMEM] * len(outputs),
        compiler_params=pltpu.CompilerParams(vmem_limit_bytes=size << 20),
        cost_estimate=pl.CostEstimate(flops=flops, bytes_accessed=4 << 20, transcendentals=0),
        name=name,
    )(*inputs)


def traded(value, axis):
    return lax.all_to_all(value, axis, split_axis=0, concat_axis=0)


def total(value):
    return jnp.sum(value.astype(F32), axis=0)


def local(image_embeds, text_features, projection, pair_step, pair_col):
    x = lax.axis_index("x")
    places = (RIGHT_AT, RIGHT2_AT, LEFT2_AT, ACROSS_AT)
    place = jnp.stack([lax.axis_index(DP), lax.axis_index("c")] + [position_of(x, at) for at in places] + [lax.axis_index(("zh", "z1"))]).astype(jnp.int32)
    image = image_embeds[0]
    features = text_features[0]
    right = shifted(image, RIGHT)
    left = shifted(image, LEFT)
    right2 = shifted(right, RIGHT2)
    left2 = shifted(left, LEFT2)
    across = shifted(right, ACROSS)

    full = (ROWS, E)
    unit, inverse, texts, acc = call(
        first_kernel,
        (place, features, projection, image, pair_step, pair_col),
        ((full, F32), ((ROWS, 128), F32), (full, BF16), (full, F32)),
        1 << 30, 24, "hidden_and_own",
    )
    acc, turned, pick_there, pick_here = call(
        second_kernel,
        (place, features, right, left, pair_step, pair_col, texts, acc),
        ((full, F32), ((D, ROWS), BF16), ((E, PICK), BF16), ((E, PICK), BF16)),
        1 << 30, 32, "near_pairs",
    )
    shape = (2, 2, SHARDS // 2, WIDTH)
    for at, block, name in ((3, right2, "far_right"), (5, across, "far_across")):
        (acc,) = call(
            functools.partial(far_kernel, at), (place, block, pair_step, pair_col, texts, acc), ((full, F32),), 1 << 28, 24, name
        )
    grad, there = call(
        third_kernel,
        (place, left2, pair_step, pair_col, texts, acc, unit, inverse, turned, pick_there),
        ((full, BF16), (shape, BF16)),
        1 << 30, 32, "far_left",
    )
    came = lax.ppermute(there, "c", [(0, 1), (1, 0)])
    here, grad_text = call(
        fourth_kernel, (grad, turned, pick_here, projection), ((shape, BF16), (full, BF16)), 1 << 30, 32, "own_half"
    )
    both = (here.astype(F32) + came.astype(F32)).astype(BF16)

    rows = total(traded(both.reshape(32, 8, WIDTH), NEAR)).astype(BF16)
    rows = (rows.astype(F32) + lax.ppermute(rows, "z1", [(0, 1), (1, 0)]).astype(F32)).astype(BF16)
    rows = traded(jnp.broadcast_to(rows[None], (4, 8, WIDTH)), "zh")
    block, square = call(block_kernel, (place, rows), (((RB, CB), F32), ((64, 8, 128), F32)), 1 << 20, 16, "block")
    square = traded(square, NEAR + ("c",))
    (block,) = call(clip_kernel, (square, block), (((RB, CB), F32),), 1 << 20, 16, "clip")
    return (grad_text[None], block)


def solution(mesh):
    split = Mesh(mesh.devices.reshape(SHAPE), AXES)
    placed = (
        P(OUTER, DP, None),
        P(OUTER, DP, None),
        P(),
        P(OUTER, None),
        P(OUTER, None),
    )
    return jax.shard_map(
        local,
        mesh=split,
        in_specs=placed,
        out_specs=(P(OUTER, DP, None), P(DP, OUTER)),
        check_vma=False,
    )
```

```python
import functools
import math

import jax
import jax.numpy as jnp
from jax import lax
from jax.experimental import pallas as pl
from jax.experimental.pallas import tpu as pltpu
from jax.sharding import Mesh, PartitionSpec as P

LOGIT_SCALE = 10.0
LOGIT_BIAS = -3.0
LOSS_SCALE = 256.0
EPSILON = 1e-06

SHARDS = 128
ROWS = 256
D = 1152
E = 1152
SHAPE = (2, 4, 2, 2, 4, 2, 2)
AXES = ("yh", "zh", "z1", "z0", "x", "yl", "c")
DP = ("yh", "zh", "z1", "z0", "x")
OUTER = ("yl", "c")
SIDE = ("yh", "x", "z0")
NEAR = ("yh", "x", "z0", "yl", "c")
RB = 9
CB = 288
MAIN = 256
REST = 32
SPLIT = RB * MAIN
WIDTH = 2688
PICK = MAIN + 128

F32 = jnp.float32
BF16 = jnp.bfloat16
VMEM = pl.BlockSpec(memory_space=pltpu.VMEM)
SMEM = pl.BlockSpec(memory_space=pltpu.SMEM)


RIGHT = (1, 1, 1, -3)
LEFT = (-1, -1, -1, -1)
RIGHT2 = (1, 1, 1, 1)
LEFT2 = (-1, -1, 3, -1)
ACROSS = (4, -4, -4, -4)
RIGHT_AT = (5, 1, 1, 1)
LEFT_AT = (3, 3, 3, 3)
RIGHT2_AT = (0, 4, 0, 0)
LEFT2_AT = (4, 0, 4, 4)
ACROSS_AT = (1, 5, 5, 5)


def shifted(value, hops):
    pairs = [(source, (source + hops[source % 4]) % SHARDS) for source in range(SHARDS)]
    return lax.ppermute(value, DP, pairs)


def position_of(x, places):
    return jnp.where(x == 0, places[0], jnp.where(x == 1, places[1], jnp.where(x == 2, places[2], places[3])))


def dot(a, b):
    return jnp.dot(a, b, preferred_element_type=F32)


def dot_t(a, b):
    return lax.dot_general(a, b, (((1,), (1,)), ((), ())), preferred_element_type=F32)


def unit_rows(values):
    values = values.astype(F32)
    inverse = lax.rsqrt(jnp.sum(values * values, axis=-1, keepdims=True) + EPSILON)
    return values * inverse, inverse


def pair_grad(step_ref, col_ref, texts, block, position):
    images = unit_rows(block)[0].astype(BF16)
    steps = step_ref[pl.ds(position, 1), :]
    cols = col_ref[pl.ds(position, 1), :]
    logits = LOGIT_SCALE * dot_t(texts, images) + LOGIT_BIAS
    rows = lax.broadcasted_iota(jnp.int32, logits.shape, 0)
    positive = (steps == position) & (cols == rows)
    scale = LOSS_SCALE * LOGIT_SCALE
    chance = 1.0 / (1.0 + jnp.exp(jnp.where(positive, logits, -logits)))
    weights = (jnp.where(positive, -scale, scale) * chance).astype(BF16)
    return dot(weights, images)


def first_kernel(
    place_ref, feat_hbm, proj_hbm, image_hbm, step_hbm, col_hbm, unit_ref, inv_ref, text_ref, acc_ref, steps_ref, cols_ref,
    feat_ref, proj_ref, image_ref, step_ref, col_ref, sems,
):
    pairs = (
        (feat_hbm, feat_ref), (proj_hbm, proj_ref), (image_hbm, image_ref), (step_hbm, step_ref), (col_hbm, col_ref)
    )
    copies = [pltpu.make_async_copy(src, dst, sems.at[i]) for i, (src, dst) in enumerate(pairs)]
    for copy in copies:
        copy.start()
    copies[0].wait()
    copies[1].wait()
    hidden = dot(feat_ref[...], proj_ref[...])
    unit, inverse = unit_rows(hidden)
    texts = unit.astype(BF16)
    unit_ref[...] = unit
    inv_ref[...] = jnp.broadcast_to(inverse, inv_ref.shape)
    text_ref[...] = texts
    for copy in copies[2:]:
        copy.wait()
    for position in range(8):
        shard = (place_ref[0] + (position + (SHARDS - 2))) & (SHARDS - 1)
        spot = pl.ds(pl.multiple_of(shard * ROWS, ROWS), ROWS)
        steps_ref[position : position + 1, :] = step_ref[:, spot]
        cols_ref[position : position + 1, :] = col_ref[:, spot]
    acc_ref[...] = pair_grad(steps_ref, cols_ref, texts, image_ref[...], 2)


def near_kernel(place_ref, right_ref, left_ref, step_ref, col_ref, text_ref, acc_ref, out_ref):
    texts = text_ref[...]
    total = acc_ref[...] + pair_grad(step_ref, col_ref, texts, right_ref[...], place_ref[1])
    out_ref[...] = total + pair_grad(step_ref, col_ref, texts, left_ref[...], 3)


def order_kernel(feat_ref, other_ref, turned_ref, pick_ref):
    spot = lax.broadcasted_iota(jnp.int32, (D, 1), 0)
    within, peer = spot >> 7, spot & (SHARDS - 1)
    yh, x, z0, z = peer >> 6, (peer >> 4) & 3, (peer >> 3) & 1, peer & 7
    source = RB * (64 * yh + 8 * z + 4 * z0 + x) + within
    lanes = lax.broadcasted_iota(jnp.int32, (D, D), 1)
    order = jnp.where(lanes == source, 1.0, 0.0).astype(BF16)
    turned_ref[0] = dot_t(order, feat_ref[...]).astype(BF16)
    turned_ref[1] = dot_t(order, other_ref[...]).astype(BF16)
    lane = lax.broadcasted_iota(jnp.int32, (1, PICK), 1)
    column = jnp.where(lane < MAIN, lane, MAIN + (lane & (REST - 1)))
    rows = lax.broadcasted_iota(jnp.int32, (E, PICK), 0)
    for block in range(4):
        pick_ref[:, block * PICK : (block + 1) * PICK] = jnp.where(rows == column + CB * block, 1.0, 0.0).astype(BF16)


def far_kernel(at, place_ref, image_ref, step_ref, col_ref, text_ref, acc_ref, out_ref):
    part = pair_grad(step_ref, col_ref, text_ref[...], image_ref[...], place_ref[at])
    out_ref[...] = acc_ref[...] + part


def last_kernel(
    place_ref, left_ref, step_ref, col_ref, text_ref, acc_ref, unit_ref, inv_ref, pick_ref, grad_ref, out_ref
):
    part = pair_grad(step_ref, col_ref, text_ref[...], left_ref[...], place_ref[3])
    total = acc_ref[...] + part
    unit = unit_ref[...]
    radial = jnp.sum(unit * total, axis=-1, keepdims=True)
    grad = (inv_ref[:, :1] * (total - unit * radial)).astype(BF16)
    grad_ref[...] = grad
    for block in range(4):
        out_ref[block] = dot(grad, pick_ref[:, block * PICK : (block + 1) * PICK]).astype(BF16)


def partial_kernel(place_ref, came_ref, turned_ref, across_ref, out_ref):
    me = place_ref[5]
    parts = [came_ref[me ^ flip] for flip in range(4)]
    group = lax.broadcasted_iota(jnp.int32, (SHARDS, 128), 1) // REST
    rest = [jnp.zeros((SHARDS, 128), F32) for _ in range(3)]
    for r in range(RB):
        rows = slice(r * SHARDS, (r + 1) * SHARDS)
        block = dot(turned_ref[0, rows, :], parts[0]) + dot(across_ref[0, rows, :], parts[1])
        block = block + dot(turned_ref[1, rows, :], parts[2]) + dot(across_ref[1, rows, :], parts[3])
        out_ref[:, r * MAIN : (r + 1) * MAIN] = block[:, :MAIN].astype(BF16)
        rest[r // 4] = jnp.where(group == r % 4, block[:, MAIN:], rest[r // 4])
    for t in range(3):
        out_ref[:, SPLIT + t * 128 : SPLIT + (t + 1) * 128] = rest[t].astype(BF16)


def text_kernel(grad_ref, proj_ref, out_ref):
    out_ref[...] = dot_t(grad_ref[...], proj_ref[...]).astype(BF16)


def block_kernel(place_ref, came_ref, block_ref, square_ref):
    rows = jnp.sum(came_ref[...].astype(F32), axis=0)
    sums = jnp.sum(rows * rows, axis=0, keepdims=True)
    square = functools.reduce(jnp.add, [sums[:, t * 128 : (t + 1) * 128] for t in range(WIDTH // 128)])
    lines = lax.broadcasted_iota(jnp.int32, (8, 128), 0)
    square = jnp.where(lines == 0, jnp.broadcast_to(square, (8, 128)), 0.0)
    square_ref[...] = jnp.broadcast_to(square[None], square_ref.shape)
    mine = lax.broadcasted_iota(jnp.int32, rows.shape, 0) == place_ref[6]
    own = jnp.sum(jnp.where(mine, rows, 0.0), axis=0, keepdims=True)
    for r in range(RB):
        block_ref[r : r + 1, :MAIN] = own[:, r * MAIN : (r + 1) * MAIN]
        block_ref[r : r + 1, MAIN:] = own[:, SPLIT + r * REST : SPLIT + (r + 1) * REST]


def clip_kernel(square_ref, block_ref, out_ref):
    square = jnp.sum(jnp.sum(square_ref[...], axis=0), keepdims=True)
    factor = jnp.minimum(1.0, math.sqrt(D * E) * lax.rsqrt(square))
    out_ref[...] = block_ref[...] * factor


def call(kernel, inputs, outputs, flops, size, name, spaces=(), scratch=()):
    specs = [SMEM if value.ndim == 1 else VMEM for value in inputs]
    for i in spaces:
        specs[i] = pl.BlockSpec(memory_space=pl.ANY)
    return pl.pallas_call(
        kernel,
        out_shape=[jax.ShapeDtypeStruct(shape, dtype) for shape, dtype in outputs],
        in_specs=specs,
        out_specs=[VMEM] * len(outputs),
        scratch_shapes=list(scratch),
        compiler_params=pltpu.CompilerParams(vmem_limit_bytes=size << 20),
        cost_estimate=pl.CostEstimate(flops=flops, bytes_accessed=4 << 20, transcendentals=0),
        name=name,
    )(*inputs)


def traded(value, axis):
    return lax.all_to_all(value, axis, split_axis=0, concat_axis=0)


def total(value):
    return jnp.sum(value.astype(F32), axis=0)


def local(image_embeds, text_features, projection, pair_step, pair_col):
    x = lax.axis_index("x")
    places = (RIGHT_AT, RIGHT2_AT, LEFT2_AT, ACROSS_AT)
    place = [lax.axis_index(DP)] + [position_of(x, at) for at in places]
    place = jnp.stack(place + [lax.axis_index(OUTER), lax.axis_index(("zh", "z1"))]).astype(jnp.int32)
    image = image_embeds[0]
    features = text_features[0]
    right = shifted(image, RIGHT)
    left = shifted(image, LEFT)
    other = lax.ppermute(features, "yl", [(0, 1), (1, 0)])

    full = (ROWS, E)
    table = (8, ROWS)
    unit, inverse, texts, acc, steps, cols = call(
        first_kernel,
        (place, features, projection, image, pair_step, pair_col),
        ((full, F32), ((ROWS, 128), F32), (full, BF16), (full, F32), (table, jnp.int32), (table, jnp.int32)),
        1 << 30, 48, "hidden_and_own", range(1, 6),
        (
            pltpu.VMEM((ROWS, D), BF16), pltpu.VMEM((D, E), BF16), pltpu.VMEM(full, BF16),
            pltpu.VMEM(pair_step.shape, jnp.int32), pltpu.VMEM(pair_col.shape, jnp.int32), pltpu.SemaphoreType.DMA((5,)),
        ),
    )
    right, left, acc = lax.optimization_barrier((right, left, acc))
    right2 = shifted(right, RIGHT2)
    left2 = shifted(left, LEFT2)
    across = shifted(right, ACROSS)
    turned, pick = call(
        order_kernel, (features, other), (((2, D, ROWS), BF16), ((E, 4 * PICK), BF16)), 1 << 30, 32, "order"
    )
    opposite = lax.ppermute(turned, "c", [(0, 1), (1, 0)])
    (acc,) = call(near_kernel, (place, right, left, steps, cols, texts, acc), ((full, F32),), 1 << 30, 24, "near_pairs")
    for at, block, name in ((2, right2, "far_right"), (4, across, "far_across")):
        (acc,) = call(
            functools.partial(far_kernel, at), (place, block, steps, cols, texts, acc), ((full, F32),), 1 << 28, 24, name
        )
    grad, columns = call(
        last_kernel,
        (place, left2, steps, cols, texts, acc, unit, inverse, pick),
        ((full, BF16), ((4, ROWS, PICK), BF16)),
        1 << 30, 32, "far_left",
    )
    columns = traded(columns, OUTER)
    (both,) = call(
        partial_kernel, (place, columns, turned, opposite), (((SHARDS, WIDTH), BF16),), 1 << 30, 32, "partial"
    )
    rows = total(traded(both.reshape(16, 8, WIDTH), SIDE)).astype(BF16)
    near = lax.ppermute(rows, "z1", [(0, 1), (1, 0)])
    (grad_text,) = call(text_kernel, (grad, projection), ((full, BF16),), 1 << 30, 24, "grad_text")
    rows = (rows.astype(F32) + near.astype(F32)).astype(BF16)
    rows = traded(jnp.broadcast_to(rows[None], (4, 8, WIDTH)), "zh")
    block, square = call(block_kernel, (place, rows), (((RB, CB), F32), ((64, 8, 128), F32)), 1 << 20, 16, "block")
    square = traded(square, NEAR)
    (block,) = call(clip_kernel, (square, block), (((RB, CB), F32),), 1 << 20, 16, "clip")
    return (grad_text[None], block)


def solution(mesh):
    split = Mesh(mesh.devices.reshape(SHAPE), AXES)
    placed = (
        P(OUTER, DP, None),
        P(OUTER, DP, None),
        P(),
        P(OUTER, None),
        P(OUTER, None),
    )
    return jax.shard_map(
        local,
        mesh=split,
        in_specs=placed,
        out_specs=(P(OUTER, DP, None), P(DP, OUTER)),
        check_vma=False,
    )
```

```python
import functools
import math

import jax
import jax.numpy as jnp
from jax import lax
from jax.experimental import pallas as pl
from jax.experimental.pallas import tpu as pltpu
from jax.sharding import Mesh, PartitionSpec as P

LOGIT_SCALE = 10.0
LOGIT_BIAS = -3.0
LOSS_SCALE = 256.0
EPSILON = 1e-06

SHARDS = 128
ROWS = 256
D = 1152
E = 1152
SHAPE = (2, 4, 2, 2, 4, 2, 2)
AXES = ("yh", "zh", "z1", "z0", "x", "yl", "c")
DP = ("yh", "zh", "z1", "z0", "x")
OUTER = ("yl", "c")
NEAR = ("yh", "yl", "x", "z0")
RB = 9
CB = 288
MAIN = 256
REST = 32
SPLIT = RB * MAIN
WIDTH = 2688
PICK = 2 * MAIN + 2 * 128

F32 = jnp.float32
BF16 = jnp.bfloat16
VMEM = pl.BlockSpec(memory_space=pltpu.VMEM)
SMEM = pl.BlockSpec(memory_space=pltpu.SMEM)


RIGHT = (1, 1, 1, -3)
LEFT = (-1, -1, -1, -1)
RIGHT2 = (1, 1, 1, 1)
LEFT2 = (-1, -1, 3, -1)
ACROSS = (4, -4, -4, -4)
RIGHT_AT = (5, 1, 1, 1)
LEFT_AT = (3, 3, 3, 3)
RIGHT2_AT = (0, 4, 0, 0)
LEFT2_AT = (4, 0, 4, 4)
ACROSS_AT = (1, 5, 5, 5)


def shifted(value, hops):
    pairs = [(source, (source + hops[source % 4]) % SHARDS) for source in range(SHARDS)]
    return lax.ppermute(value, DP, pairs)


def position_of(x, places):
    return jnp.where(x == 0, places[0], jnp.where(x == 1, places[1], jnp.where(x == 2, places[2], places[3])))


def dot(a, b):
    return jnp.dot(a, b, preferred_element_type=F32)


def dot_t(a, b):
    return lax.dot_general(a, b, (((1,), (1,)), ((), ())), preferred_element_type=F32)


def unit_rows(values):
    values = values.astype(F32)
    inverse = lax.rsqrt(jnp.sum(values * values, axis=-1, keepdims=True) + EPSILON)
    return values * inverse, inverse


def pair_grad(step_ref, col_ref, texts, block, position):
    images = unit_rows(block)[0].astype(BF16)
    steps = step_ref[pl.ds(position, 1), :]
    cols = col_ref[pl.ds(position, 1), :]
    logits = LOGIT_SCALE * dot_t(texts, images) + LOGIT_BIAS
    rows = lax.broadcasted_iota(jnp.int32, logits.shape, 0)
    positive = (steps == position) & (cols == rows)
    scale = LOSS_SCALE * LOGIT_SCALE
    chance = 1.0 / (1.0 + jnp.exp(jnp.where(positive, logits, -logits)))
    weights = (jnp.where(positive, -scale, scale) * chance).astype(BF16)
    return dot(weights, images)


def first_kernel(
    place_ref, feat_hbm, proj_hbm, image_hbm, step_hbm, col_hbm, unit_ref, inv_ref, text_ref, acc_ref, steps_ref, cols_ref,
    feat_ref, proj_ref, image_ref, step_ref, col_ref, sems,
):
    pairs = (
        (feat_hbm, feat_ref), (proj_hbm, proj_ref), (image_hbm, image_ref), (step_hbm, step_ref), (col_hbm, col_ref)
    )
    copies = [pltpu.make_async_copy(src, dst, sems.at[i]) for i, (src, dst) in enumerate(pairs)]
    for copy in copies:
        copy.start()
    copies[0].wait()
    copies[1].wait()
    hidden = dot(feat_ref[...], proj_ref[...])
    unit, inverse = unit_rows(hidden)
    texts = unit.astype(BF16)
    unit_ref[...] = unit
    inv_ref[...] = jnp.broadcast_to(inverse, inv_ref.shape)
    text_ref[...] = texts
    for copy in copies[2:]:
        copy.wait()
    for position in range(8):
        shard = (place_ref[0] + (position + (SHARDS - 2))) & (SHARDS - 1)
        spot = pl.ds(pl.multiple_of(shard * ROWS, ROWS), ROWS)
        steps_ref[position : position + 1, :] = step_ref[:, spot]
        cols_ref[position : position + 1, :] = col_ref[:, spot]
    acc_ref[...] = pair_grad(steps_ref, cols_ref, texts, image_ref[...], 2)


def near_kernel(place_ref, right_ref, left_ref, step_ref, col_ref, text_ref, acc_ref, out_ref):
    texts = text_ref[...]
    total = acc_ref[...] + pair_grad(step_ref, col_ref, texts, right_ref[...], place_ref[1])
    out_ref[...] = total + pair_grad(step_ref, col_ref, texts, left_ref[...], 3)


def column_of(lane, core):
    tail = lane - 2 * MAIN
    pair = jnp.where(lane < 2 * MAIN, lane >> 8, tail >> 7)
    inside = jnp.where(lane < 2 * MAIN, lane & (MAIN - 1), MAIN + (lane & (REST - 1)))
    return CB * (2 * pair + core) + inside


def order_kernel(place_ref, feat_ref, turned_ref, there_ref, here_ref):
    spot = lax.broadcasted_iota(jnp.int32, (D, 1), 0)
    within, peer = spot >> 7, spot & (SHARDS - 1)
    yh, x, z0, z = peer >> 6, (peer >> 4) & 3, (peer >> 3) & 1, peer & 7
    source = RB * (64 * yh + 8 * z + 4 * z0 + x) + within
    lanes = lax.broadcasted_iota(jnp.int32, (D, D), 1)
    order = jnp.where(lanes == source, 1.0, 0.0).astype(BF16)
    turned_ref[...] = dot_t(order, feat_ref[...]).astype(BF16)
    core = place_ref[5]
    lane = lax.broadcasted_iota(jnp.int32, (1, PICK), 1)
    rows = lax.broadcasted_iota(jnp.int32, (E, PICK), 0)
    there_ref[...] = jnp.where(rows == column_of(lane, 1 - core), 1.0, 0.0).astype(BF16)
    here_ref[...] = jnp.where(rows == column_of(lane, core), 1.0, 0.0).astype(BF16)


def far_kernel(at, place_ref, image_ref, step_ref, col_ref, text_ref, acc_ref, out_ref):
    part = pair_grad(step_ref, col_ref, text_ref[...], image_ref[...], place_ref[at])
    out_ref[...] = acc_ref[...] + part


def last_kernel(
    place_ref, left_ref, step_ref, col_ref, text_ref, acc_ref, unit_ref, inv_ref, pick_ref, grad_ref, out_ref
):
    part = pair_grad(step_ref, col_ref, text_ref[...], left_ref[...], place_ref[3])
    total = acc_ref[...] + part
    unit = unit_ref[...]
    radial = jnp.sum(unit * total, axis=-1, keepdims=True)
    grad = (inv_ref[:, :1] * (total - unit * radial)).astype(BF16)
    grad_ref[...] = grad
    out_ref[...] = dot(grad, pick_ref[...]).astype(BF16)


def own_kernel(grad_ref, pick_ref, out_ref):
    out_ref[...] = dot(grad_ref[...], pick_ref[...]).astype(BF16)


def partial_kernel(own_ref, came_ref, turned_ref, opposite_ref, out_ref):
    half = SHARDS // 2
    group = lax.broadcasted_iota(jnp.int32, (SHARDS, 128), 1) // REST
    rest = [[jnp.zeros((SHARDS, 128), F32) for _ in range(3)] for _ in range(2)]

    def put(pair, lanes, value):
        value = value.astype(BF16)
        for yh in range(2):
            out_ref[yh, pair, :, lanes] = value[yh * half : (yh + 1) * half]

    for r in range(RB):
        rows = slice(r * SHARDS, (r + 1) * SHARDS)
        block = dot(turned_ref[rows, :], own_ref[...]) + dot(opposite_ref[rows, :], came_ref[...])
        for pair in range(2):
            put(pair, slice(r * MAIN, (r + 1) * MAIN), block[:, pair * MAIN : (pair + 1) * MAIN])
            tail = block[:, 2 * MAIN + pair * 128 : 2 * MAIN + (pair + 1) * 128]
            rest[pair][r // 4] = jnp.where(group == r % 4, tail, rest[pair][r // 4])
    for pair in range(2):
        for t in range(3):
            put(pair, slice(SPLIT + t * 128, SPLIT + (t + 1) * 128), rest[pair][t])


def text_kernel(grad_ref, proj_ref, out_ref):
    out_ref[...] = dot_t(grad_ref[...], proj_ref[...]).astype(BF16)


def block_kernel(place_ref, came_ref, block_ref, square_ref):
    rows = jnp.sum(came_ref[...].astype(F32), axis=0)
    sums = jnp.sum(rows * rows, axis=0, keepdims=True)
    square = functools.reduce(jnp.add, [sums[:, t * 128 : (t + 1) * 128] for t in range(WIDTH // 128)])
    lines = lax.broadcasted_iota(jnp.int32, (8, 128), 0)
    square = jnp.where(lines == 0, jnp.broadcast_to(square, (8, 128)), 0.0)
    square_ref[...] = jnp.broadcast_to(square[None], square_ref.shape)
    mine = lax.broadcasted_iota(jnp.int32, rows.shape, 0) == place_ref[6]
    own = jnp.sum(jnp.where(mine, rows, 0.0), axis=0, keepdims=True)
    for r in range(RB):
        block_ref[r : r + 1, :MAIN] = own[:, r * MAIN : (r + 1) * MAIN]
        block_ref[r : r + 1, MAIN:] = own[:, SPLIT + r * REST : SPLIT + (r + 1) * REST]


def clip_kernel(square_ref, block_ref, out_ref):
    square = jnp.sum(jnp.sum(square_ref[...], axis=0), keepdims=True)
    factor = jnp.minimum(1.0, math.sqrt(D * E) * lax.rsqrt(square))
    out_ref[...] = block_ref[...] * factor


def call(kernel, inputs, outputs, flops, size, name, spaces=(), scratch=()):
    specs = [SMEM if value.ndim == 1 else VMEM for value in inputs]
    for i in spaces:
        specs[i] = pl.BlockSpec(memory_space=pl.ANY)
    return pl.pallas_call(
        kernel,
        out_shape=[jax.ShapeDtypeStruct(shape, dtype) for shape, dtype in outputs],
        in_specs=specs,
        out_specs=[VMEM] * len(outputs),
        scratch_shapes=list(scratch),
        compiler_params=pltpu.CompilerParams(vmem_limit_bytes=size << 20),
        cost_estimate=pl.CostEstimate(flops=flops, bytes_accessed=4 << 20, transcendentals=0),
        name=name,
    )(*inputs)


def traded(value, axis):
    return lax.all_to_all(value, axis, split_axis=0, concat_axis=0)


def total(value):
    return jnp.sum(value.astype(F32), axis=0)


def local(image_embeds, text_features, projection, pair_step, pair_col):
    x = lax.axis_index("x")
    places = (RIGHT_AT, RIGHT2_AT, LEFT2_AT, ACROSS_AT)
    place = [lax.axis_index(DP)] + [position_of(x, at) for at in places]
    place = jnp.stack(place + [lax.axis_index("c"), lax.axis_index(("zh", "z1"))]).astype(jnp.int32)
    image = image_embeds[0]
    features = text_features[0]
    right = shifted(image, RIGHT)
    left = shifted(image, LEFT)
    right2 = shifted(right, RIGHT2)
    left2 = shifted(left, LEFT2)
    across = shifted(right, ACROSS)

    full = (ROWS, E)
    table = (8, ROWS)
    unit, inverse, texts, acc, steps, cols = call(
        first_kernel,
        (place, features, projection, image, pair_step, pair_col),
        ((full, F32), ((ROWS, 128), F32), (full, BF16), (full, F32), (table, jnp.int32), (table, jnp.int32)),
        1 << 30, 48, "hidden_and_own", range(1, 6),
        (
            pltpu.VMEM((ROWS, D), BF16), pltpu.VMEM((D, E), BF16), pltpu.VMEM(full, BF16),
            pltpu.VMEM(pair_step.shape, jnp.int32), pltpu.VMEM(pair_col.shape, jnp.int32), pltpu.SemaphoreType.DMA((5,)),
        ),
    )
    turned, pick_there, pick_here = call(
        order_kernel, (place, features), (((D, ROWS), BF16), ((E, PICK), BF16), ((E, PICK), BF16)), 1 << 30, 32, "order"
    )
    swap = [(0, 1), (1, 0)]
    opposite = lax.ppermute(turned, "c", swap)
    (acc,) = call(near_kernel, (place, right, left, steps, cols, texts, acc), ((full, F32),), 1 << 30, 24, "near_pairs")
    for at, block, name in ((2, right2, "far_right"), (4, across, "far_across")):
        (acc,) = call(
            functools.partial(far_kernel, at), (place, block, steps, cols, texts, acc), ((full, F32),), 1 << 28, 24, name
        )
    grad, columns = call(
        last_kernel,
        (place, left2, steps, cols, texts, acc, unit, inverse, pick_there),
        ((full, BF16), ((ROWS, PICK), BF16)),
        1 << 30, 32, "far_left",
    )
    columns = lax.ppermute(columns, "c", swap)
    (own,) = call(own_kernel, (grad, pick_here), (((ROWS, PICK), BF16),), 1 << 28, 24, "own_columns")
    (both,) = call(
        partial_kernel, (own, columns, turned, opposite), (((2, 2, SHARDS // 2, WIDTH), BF16),), 1 << 30, 32, "partial"
    )
    rows = total(traded(both.reshape(32, 8, WIDTH), NEAR)).astype(BF16)
    near = lax.ppermute(rows, "z1", swap)
    (grad_text,) = call(text_kernel, (grad, projection), ((full, BF16),), 1 << 30, 24, "grad_text")
    rows = (rows.astype(F32) + near.astype(F32)).astype(BF16)
    rows = traded(jnp.broadcast_to(rows[None], (4, 8, WIDTH)), "zh")
    block, square = call(block_kernel, (place, rows), (((RB, CB), F32), ((64, 8, 128), F32)), 1 << 20, 16, "block")
    square = traded(square, NEAR + ("c",))
    (block,) = call(clip_kernel, (square, block), (((RB, CB), F32),), 1 << 20, 16, "clip")
    return (grad_text[None], block)


def solution(mesh):
    split = Mesh(mesh.devices.reshape(SHAPE), AXES)
    placed = (
        P(OUTER, DP, None),
        P(OUTER, DP, None),
        P(),
        P(OUTER, None),
        P(OUTER, None),
    )
    return jax.shard_map(
        local,
        mesh=split,
        in_specs=placed,
        out_specs=(P(OUTER, DP, None), P(DP, OUTER)),
        check_vma=False,
    )
```

```python
import functools
import math

import jax
import jax.numpy as jnp
from jax import lax
from jax.experimental import pallas as pl
from jax.experimental.pallas import tpu as pltpu
from jax.sharding import Mesh, PartitionSpec as P

LOGIT_SCALE = 10.0
LOGIT_BIAS = -3.0
LOSS_SCALE = 256.0
EPSILON = 1e-06

SHARDS = 128
ROWS = 256
D = 1152
E = 1152
SHAPE = (2, 4, 2, 2, 4, 2, 2)
AXES = ("yh", "zh", "z1", "z0", "x", "yl", "c")
DP = ("yh", "zh", "z1", "z0", "x")
OUTER = ("yl", "c")
NEAR = ("yh", "yl", "x", "z0")
RB = 9
CB = 288
MAIN = 256
REST = 32
SPLIT = RB * MAIN
WIDTH = 2688
PICK = 2 * MAIN + 2 * 128

F32 = jnp.float32
BF16 = jnp.bfloat16
VMEM = pl.BlockSpec(memory_space=pltpu.VMEM)
SMEM = pl.BlockSpec(memory_space=pltpu.SMEM)


RIGHT = (1, 1, 1, -3)
LEFT = (-1, -1, -1, -1)
RIGHT2 = (1, 1, 1, 1)
LEFT2 = (-1, -1, 3, -1)
ACROSS = (4, -4, -4, -4)
RIGHT_AT = (5, 1, 1, 1)
LEFT_AT = (3, 3, 3, 3)
RIGHT2_AT = (0, 4, 0, 0)
LEFT2_AT = (4, 0, 4, 4)
ACROSS_AT = (1, 5, 5, 5)


def shifted(value, hops):
    pairs = [(source, (source + hops[source % 4]) % SHARDS) for source in range(SHARDS)]
    return lax.ppermute(value, DP, pairs)


def position_of(x, places):
    return jnp.where(x == 0, places[0], jnp.where(x == 1, places[1], jnp.where(x == 2, places[2], places[3])))


def dot(a, b):
    return jnp.dot(a, b, preferred_element_type=F32)


def dot_t(a, b):
    return lax.dot_general(a, b, (((1,), (1,)), ((), ())), preferred_element_type=F32)


def unit_rows(values):
    values = values.astype(F32)
    inverse = lax.rsqrt(jnp.sum(values * values, axis=-1, keepdims=True) + EPSILON)
    return values * inverse, inverse


def pair_grad(step_ref, col_ref, texts, block, position):
    images = unit_rows(block)[0].astype(BF16)
    steps = step_ref[pl.ds(position, 1), :]
    cols = col_ref[pl.ds(position, 1), :]
    logits = LOGIT_SCALE * dot_t(texts, images) + LOGIT_BIAS
    rows = lax.broadcasted_iota(jnp.int32, logits.shape, 0)
    positive = (steps == position) & (cols == rows)
    scale = LOSS_SCALE * LOGIT_SCALE
    chance = 1.0 / (1.0 + jnp.exp(jnp.where(positive, logits, -logits)))
    weights = (jnp.where(positive, -scale, scale) * chance).astype(BF16)
    return dot(weights, images)


def first_kernel(
    place_ref, feat_hbm, proj_hbm, image_hbm, step_hbm, col_hbm, unit_ref, inv_ref, text_ref, acc_ref, steps_ref, cols_ref,
    feat_ref, proj_ref, image_ref, step_ref, col_ref, sems,
):
    pairs = (
        (feat_hbm, feat_ref), (proj_hbm, proj_ref), (image_hbm, image_ref), (step_hbm, step_ref), (col_hbm, col_ref)
    )
    copies = [pltpu.make_async_copy(src, dst, sems.at[i]) for i, (src, dst) in enumerate(pairs)]
    for copy in copies:
        copy.start()
    copies[0].wait()
    copies[1].wait()
    hidden = dot(feat_ref[...], proj_ref[...])
    unit, inverse = unit_rows(hidden)
    texts = unit.astype(BF16)
    unit_ref[...] = unit
    inv_ref[...] = jnp.broadcast_to(inverse, inv_ref.shape)
    text_ref[...] = texts
    for copy in copies[2:]:
        copy.wait()
    for position in range(8):
        shard = (place_ref[0] + (position + (SHARDS - 2))) & (SHARDS - 1)
        spot = pl.ds(pl.multiple_of(shard * ROWS, ROWS), ROWS)
        steps_ref[position : position + 1, :] = step_ref[:, spot]
        cols_ref[position : position + 1, :] = col_ref[:, spot]
    acc_ref[...] = pair_grad(steps_ref, cols_ref, texts, image_ref[...], 2)


def near_kernel(place_ref, right_ref, left_ref, step_ref, col_ref, text_ref, acc_ref, out_ref):
    texts = text_ref[...]
    total = acc_ref[...] + pair_grad(step_ref, col_ref, texts, right_ref[...], place_ref[1])
    out_ref[...] = total + pair_grad(step_ref, col_ref, texts, left_ref[...], 3)


def column_of(lane, core):
    tail = lane - 2 * MAIN
    pair = jnp.where(lane < 2 * MAIN, lane >> 8, tail >> 7)
    inside = jnp.where(lane < 2 * MAIN, lane & (MAIN - 1), MAIN + (lane & (REST - 1)))
    return CB * (2 * pair + core) + inside


def order_kernel(place_ref, feat_ref, turned_ref, there_ref, here_ref):
    spot = lax.broadcasted_iota(jnp.int32, (D, 1), 0)
    within, peer = spot >> 7, spot & (SHARDS - 1)
    yh, x, z0, z = peer >> 6, (peer >> 4) & 3, (peer >> 3) & 1, peer & 7
    source = RB * (64 * yh + 8 * z + 4 * z0 + x) + within
    lanes = lax.broadcasted_iota(jnp.int32, (D, D), 1)
    order = jnp.where(lanes == source, 1.0, 0.0).astype(BF16)
    turned_ref[...] = dot_t(order, feat_ref[...]).astype(BF16)
    core = place_ref[5]
    lane = lax.broadcasted_iota(jnp.int32, (1, PICK), 1)
    rows = lax.broadcasted_iota(jnp.int32, (E, PICK), 0)
    there_ref[...] = jnp.where(rows == column_of(lane, 1 - core), 1.0, 0.0).astype(BF16)
    here_ref[...] = jnp.where(rows == column_of(lane, core), 1.0, 0.0).astype(BF16)


def far_kernel(at, place_ref, image_ref, step_ref, col_ref, text_ref, acc_ref, out_ref):
    part = pair_grad(step_ref, col_ref, text_ref[...], image_ref[...], place_ref[at])
    out_ref[...] = acc_ref[...] + part


def last_kernel(
    place_ref, left_ref, step_ref, col_ref, text_ref, acc_ref, unit_ref, inv_ref, pick_ref, grad_ref, out_ref
):
    part = pair_grad(step_ref, col_ref, text_ref[...], left_ref[...], place_ref[3])
    total = acc_ref[...] + part
    unit = unit_ref[...]
    radial = jnp.sum(unit * total, axis=-1, keepdims=True)
    grad = (inv_ref[:, :1] * (total - unit * radial)).astype(BF16)
    grad_ref[...] = grad
    out_ref[...] = dot(grad, pick_ref[...]).astype(BF16)


def own_kernel(grad_ref, pick_ref, proj_ref, out_ref, text_ref):
    out_ref[...] = dot(grad_ref[...], pick_ref[...]).astype(BF16)
    text_ref[...] = dot_t(grad_ref[...], proj_ref[...]).astype(BF16)


def partial_kernel(own_ref, came_ref, turned_ref, opposite_ref, out_ref):
    half = SHARDS // 2
    group = lax.broadcasted_iota(jnp.int32, (SHARDS, 128), 1) // REST
    rest = [[jnp.zeros((SHARDS, 128), F32) for _ in range(3)] for _ in range(2)]

    def put(pair, lanes, value):
        value = value.astype(BF16)
        for yh in range(2):
            out_ref[yh, pair, :, lanes] = value[yh * half : (yh + 1) * half]

    for r in range(RB):
        rows = slice(r * SHARDS, (r + 1) * SHARDS)
        block = dot(turned_ref[rows, :], own_ref[...]) + dot(opposite_ref[rows, :], came_ref[...])
        for pair in range(2):
            put(pair, slice(r * MAIN, (r + 1) * MAIN), block[:, pair * MAIN : (pair + 1) * MAIN])
            tail = block[:, 2 * MAIN + pair * 128 : 2 * MAIN + (pair + 1) * 128]
            rest[pair][r // 4] = jnp.where(group == r % 4, tail, rest[pair][r // 4])
    for pair in range(2):
        for t in range(3):
            put(pair, slice(SPLIT + t * 128, SPLIT + (t + 1) * 128), rest[pair][t])


def block_kernel(place_ref, came_ref, block_ref, square_ref):
    rows = jnp.sum(came_ref[...].astype(F32), axis=0)
    sums = jnp.sum(rows * rows, axis=0, keepdims=True)
    square = functools.reduce(jnp.add, [sums[:, t * 128 : (t + 1) * 128] for t in range(WIDTH // 128)])
    lines = lax.broadcasted_iota(jnp.int32, (8, 128), 0)
    square = jnp.where(lines == 0, jnp.broadcast_to(square, (8, 128)), 0.0)
    square_ref[...] = jnp.broadcast_to(square[None], square_ref.shape)
    mine = lax.broadcasted_iota(jnp.int32, rows.shape, 0) == place_ref[6]
    own = jnp.sum(jnp.where(mine, rows, 0.0), axis=0, keepdims=True)
    for r in range(RB):
        block_ref[r : r + 1, :MAIN] = own[:, r * MAIN : (r + 1) * MAIN]
        block_ref[r : r + 1, MAIN:] = own[:, SPLIT + r * REST : SPLIT + (r + 1) * REST]


def clip_kernel(square_ref, block_ref, out_ref):
    square = jnp.sum(jnp.sum(square_ref[...], axis=0), keepdims=True)
    factor = jnp.minimum(1.0, math.sqrt(D * E) * lax.rsqrt(square))
    out_ref[...] = block_ref[...] * factor


def call(kernel, inputs, outputs, flops, size, name, spaces=(), scratch=()):
    specs = [SMEM if value.ndim == 1 else VMEM for value in inputs]
    for i in spaces:
        specs[i] = pl.BlockSpec(memory_space=pl.ANY)
    return pl.pallas_call(
        kernel,
        out_shape=[jax.ShapeDtypeStruct(shape, dtype) for shape, dtype in outputs],
        in_specs=specs,
        out_specs=[VMEM] * len(outputs),
        scratch_shapes=list(scratch),
        compiler_params=pltpu.CompilerParams(vmem_limit_bytes=size << 20),
        cost_estimate=pl.CostEstimate(flops=flops, bytes_accessed=4 << 20, transcendentals=0),
        name=name,
    )(*inputs)


def traded(value, axis):
    return lax.all_to_all(value, axis, split_axis=0, concat_axis=0)


def total(value):
    return jnp.sum(value.astype(F32), axis=0)


def local(image_embeds, text_features, projection, pair_step, pair_col):
    x = lax.axis_index("x")
    places = (RIGHT_AT, RIGHT2_AT, LEFT2_AT, ACROSS_AT)
    place = [lax.axis_index(DP)] + [position_of(x, at) for at in places]
    place = jnp.stack(place + [lax.axis_index("c"), lax.axis_index(("zh", "z1"))]).astype(jnp.int32)
    image = image_embeds[0]
    features = text_features[0]
    right = shifted(image, RIGHT)
    left = shifted(image, LEFT)
    right2 = shifted(right, RIGHT2)
    left2 = shifted(left, LEFT2)
    across = shifted(right, ACROSS)

    full = (ROWS, E)
    table = (8, ROWS)
    unit, inverse, texts, acc, steps, cols = call(
        first_kernel,
        (place, features, projection, image, pair_step, pair_col),
        ((full, F32), ((ROWS, 128), F32), (full, BF16), (full, F32), (table, jnp.int32), (table, jnp.int32)),
        1 << 30, 48, "hidden_and_own", range(1, 6),
        (
            pltpu.VMEM((ROWS, D), BF16), pltpu.VMEM((D, E), BF16), pltpu.VMEM(full, BF16),
            pltpu.VMEM(pair_step.shape, jnp.int32), pltpu.VMEM(pair_col.shape, jnp.int32), pltpu.SemaphoreType.DMA((5,)),
        ),
    )
    turned, pick_there, pick_here = call(
        order_kernel, (place, features), (((D, ROWS), BF16), ((E, PICK), BF16), ((E, PICK), BF16)), 1 << 30, 32, "order"
    )
    swap = [(0, 1), (1, 0)]
    opposite = lax.ppermute(turned, "c", swap)
    (acc,) = call(near_kernel, (place, right, left, steps, cols, texts, acc), ((full, F32),), 1 << 30, 24, "near_pairs")
    for at, block, name in ((2, right2, "far_right"), (4, across, "far_across")):
        (acc,) = call(
            functools.partial(far_kernel, at), (place, block, steps, cols, texts, acc), ((full, F32),), 1 << 28, 24, name
        )
    grad, columns = call(
        last_kernel,
        (place, left2, steps, cols, texts, acc, unit, inverse, pick_there),
        ((full, BF16), ((ROWS, PICK), BF16)),
        1 << 30, 32, "far_left",
    )
    columns = lax.ppermute(columns, "c", swap)
    own, grad_text = call(
        own_kernel, (grad, pick_here, projection), (((ROWS, PICK), BF16), (full, BF16)), 1 << 28, 24, "own_columns"
    )
    (both,) = call(
        partial_kernel, (own, columns, turned, opposite), (((2, 2, SHARDS // 2, WIDTH), BF16),), 1 << 30, 32, "partial"
    )
    rows = total(traded(both.reshape(32, 8, WIDTH), NEAR)).astype(BF16)
    near = lax.ppermute(rows, "z1", swap)
    rows = (rows.astype(F32) + near.astype(F32)).astype(BF16)
    rows = traded(jnp.broadcast_to(rows[None], (4, 8, WIDTH)), "zh")
    block, square = call(block_kernel, (place, rows), (((RB, CB), F32), ((64, 8, 128), F32)), 1 << 20, 16, "block")
    square = traded(square, NEAR + ("c",))
    (block,) = call(clip_kernel, (square, block), (((RB, CB), F32),), 1 << 20, 16, "clip")
    return (grad_text[None], block)


def solution(mesh):
    split = Mesh(mesh.devices.reshape(SHAPE), AXES)
    placed = (
        P(OUTER, DP, None),
        P(OUTER, DP, None),
        P(),
        P(OUTER, None),
        P(OUTER, None),
    )
    return jax.shard_map(
        local,
        mesh=split,
        in_specs=placed,
        out_specs=(P(OUTER, DP, None), P(DP, OUTER)),
        check_vma=False,
    )
```

```python
import functools
import math

import jax
import jax.numpy as jnp
from jax import lax
from jax.experimental import pallas as pl
from jax.experimental.pallas import tpu as pltpu
from jax.sharding import Mesh, PartitionSpec as P

LOGIT_SCALE = 10.0
LOGIT_BIAS = -3.0
LOSS_SCALE = 256.0
EPSILON = 1e-06

SHARDS = 128
ROWS = 256
D = 1152
E = 1152
SHAPE = (2, 4, 2, 2, 4, 2, 2)
AXES = ("yh", "zh", "z1", "z0", "x", "yl", "c")
DP = ("yh", "zh", "z1", "z0", "x")
OUTER = ("yl", "c")
NEAR = ("yh", "yl", "x", "z0")
RB = 9
CB = 288
MAIN = 256
REST = 32
SPLIT = RB * MAIN
WIDTH = 2688
PICK = 2 * MAIN + 2 * 128

F32 = jnp.float32
BF16 = jnp.bfloat16
VMEM = pl.BlockSpec(memory_space=pltpu.VMEM)
SMEM = pl.BlockSpec(memory_space=pltpu.SMEM)


RIGHT = (1, 1, 1, -3)
LEFT = (-1, -1, -1, -1)
RIGHT2 = (1, 1, 1, 1)
LEFT2 = (-1, -1, 3, -1)
ACROSS = (4, -4, -4, -4)
RIGHT_AT = (5, 1, 1, 1)
LEFT_AT = (3, 3, 3, 3)
RIGHT2_AT = (0, 4, 0, 0)
LEFT2_AT = (4, 0, 4, 4)
ACROSS_AT = (1, 5, 5, 5)


def shifted(value, hops):
    pairs = [(source, (source + hops[source % 4]) % SHARDS) for source in range(SHARDS)]
    return lax.ppermute(value, DP, pairs)


def position_of(x, places):
    return jnp.where(x == 0, places[0], jnp.where(x == 1, places[1], jnp.where(x == 2, places[2], places[3])))


def dot(a, b):
    return jnp.dot(a, b, preferred_element_type=F32)


def dot_t(a, b):
    return lax.dot_general(a, b, (((1,), (1,)), ((), ())), preferred_element_type=F32)


def unit_rows(values):
    values = values.astype(F32)
    inverse = lax.rsqrt(jnp.sum(values * values, axis=-1, keepdims=True) + EPSILON)
    return values * inverse, inverse


def pair_grad(step_ref, col_ref, texts, block, position):
    images = unit_rows(block)[0].astype(BF16)
    steps = step_ref[pl.ds(position, 1), :]
    cols = col_ref[pl.ds(position, 1), :]
    logits = LOGIT_SCALE * dot_t(texts, images) + LOGIT_BIAS
    rows = lax.broadcasted_iota(jnp.int32, logits.shape, 0)
    positive = (steps == position) & (cols == rows)
    scale = LOSS_SCALE * LOGIT_SCALE
    chance = 1.0 / (1.0 + jnp.exp(jnp.where(positive, logits, -logits)))
    weights = (jnp.where(positive, -scale, scale) * chance).astype(BF16)
    return dot(weights, images)


def first_kernel(
    place_ref, feat_hbm, proj_hbm, image_hbm, step_hbm, col_hbm, unit_ref, inv_ref, text_ref, acc_ref, steps_ref, cols_ref,
    feat_ref, proj_ref, image_ref, step_ref, col_ref, sems,
):
    pairs = (
        (feat_hbm, feat_ref), (proj_hbm, proj_ref), (image_hbm, image_ref), (step_hbm, step_ref), (col_hbm, col_ref)
    )
    copies = [pltpu.make_async_copy(src, dst, sems.at[i]) for i, (src, dst) in enumerate(pairs)]
    for copy in copies:
        copy.start()
    copies[0].wait()
    copies[1].wait()
    hidden = dot(feat_ref[...], proj_ref[...])
    unit, inverse = unit_rows(hidden)
    texts = unit.astype(BF16)
    unit_ref[...] = unit
    inv_ref[...] = jnp.broadcast_to(inverse, inv_ref.shape)
    text_ref[...] = texts
    for copy in copies[2:]:
        copy.wait()
    for position in range(8):
        shard = (place_ref[0] + (position + (SHARDS - 2))) & (SHARDS - 1)
        spot = pl.ds(pl.multiple_of(shard * ROWS, ROWS), ROWS)
        steps_ref[position : position + 1, :] = step_ref[:, spot]
        cols_ref[position : position + 1, :] = col_ref[:, spot]
    acc_ref[...] = pair_grad(steps_ref, cols_ref, texts, image_ref[...], 2)


def near_kernel(place_ref, right_ref, left_ref, step_ref, col_ref, text_ref, acc_ref, out_ref):
    texts = text_ref[...]
    total = acc_ref[...] + pair_grad(step_ref, col_ref, texts, right_ref[...], place_ref[1])
    out_ref[...] = total + pair_grad(step_ref, col_ref, texts, left_ref[...], 3)


def column_of(lane, core):
    tail = lane - 2 * MAIN
    pair = jnp.where(lane < 2 * MAIN, lane >> 8, tail >> 7)
    inside = jnp.where(lane < 2 * MAIN, lane & (MAIN - 1), MAIN + (lane & (REST - 1)))
    return CB * (2 * pair + core) + inside


def order_kernel(place_ref, feat_ref, turned_ref, there_ref, here_ref):
    spot = lax.broadcasted_iota(jnp.int32, (D, 1), 0)
    within, peer = spot >> 7, spot & (SHARDS - 1)
    yh, x, z0, z = peer >> 6, (peer >> 4) & 3, (peer >> 3) & 1, peer & 7
    source = RB * (64 * yh + 8 * z + 4 * z0 + x) + within
    lanes = lax.broadcasted_iota(jnp.int32, (D, D), 1)
    order = jnp.where(lanes == source, 1.0, 0.0).astype(BF16)
    turned_ref[...] = dot_t(order, feat_ref[...]).astype(BF16)
    core = place_ref[5]
    lane = lax.broadcasted_iota(jnp.int32, (1, PICK), 1)
    rows = lax.broadcasted_iota(jnp.int32, (E, PICK), 0)
    there_ref[...] = jnp.where(rows == column_of(lane, 1 - core), 1.0, 0.0).astype(BF16)
    here_ref[...] = jnp.where(rows == column_of(lane, core), 1.0, 0.0).astype(BF16)


def far_kernel(at, place_ref, image_ref, step_ref, col_ref, text_ref, acc_ref, out_ref):
    part = pair_grad(step_ref, col_ref, text_ref[...], image_ref[...], place_ref[at])
    out_ref[...] = acc_ref[...] + part


def last_kernel(
    place_ref, left_ref, step_ref, col_ref, text_ref, acc_ref, unit_ref, inv_ref, pick_ref, grad_ref, out_ref
):
    part = pair_grad(step_ref, col_ref, text_ref[...], left_ref[...], place_ref[3])
    total = acc_ref[...] + part
    unit = unit_ref[...]
    radial = jnp.sum(unit * total, axis=-1, keepdims=True)
    grad = (inv_ref[:, :1] * (total - unit * radial)).astype(BF16)
    grad_ref[...] = grad
    out_ref[...] = dot(grad, pick_ref[...]).astype(BF16)


def own_kernel(grad_ref, pick_ref, proj_ref, out_ref, text_ref):
    out_ref[...] = dot(grad_ref[...], pick_ref[...]).astype(BF16)
    text_ref[...] = dot_t(grad_ref[...], proj_ref[...]).astype(BF16)


def partial_kernel(own_ref, came_ref, turned_ref, opposite_ref, out_ref):
    half = SHARDS // 2
    group = lax.broadcasted_iota(jnp.int32, (SHARDS, 128), 1) // REST
    rest = [[jnp.zeros((SHARDS, 128), F32) for _ in range(3)] for _ in range(2)]

    def put(pair, lanes, value):
        value = value.astype(BF16)
        for yh in range(2):
            out_ref[yh, pair, :, lanes] = value[yh * half : (yh + 1) * half]

    for r in range(RB):
        rows = slice(r * SHARDS, (r + 1) * SHARDS)
        block = dot(turned_ref[rows, :], own_ref[...]) + dot(opposite_ref[rows, :], came_ref[...])
        for pair in range(2):
            put(pair, slice(r * MAIN, (r + 1) * MAIN), block[:, pair * MAIN : (pair + 1) * MAIN])
            tail = block[:, 2 * MAIN + pair * 128 : 2 * MAIN + (pair + 1) * 128]
            rest[pair][r // 4] = jnp.where(group == r % 4, tail, rest[pair][r // 4])
    for pair in range(2):
        for t in range(3):
            put(pair, slice(SPLIT + t * 128, SPLIT + (t + 1) * 128), rest[pair][t])


def block_kernel(place_ref, came_ref, block_ref, square_ref):
    rows = jnp.sum(came_ref[...].astype(F32), axis=0)
    sums = jnp.sum(rows * rows, axis=0, keepdims=True)
    square = functools.reduce(jnp.add, [sums[:, t * 128 : (t + 1) * 128] for t in range(WIDTH // 128)])
    lines = lax.broadcasted_iota(jnp.int32, (8, 128), 0)
    square = jnp.where(lines == 0, jnp.broadcast_to(square, (8, 128)), 0.0)
    square_ref[...] = jnp.broadcast_to(square[None], square_ref.shape)
    mine = lax.broadcasted_iota(jnp.int32, rows.shape, 0) == place_ref[6]
    own = jnp.sum(jnp.where(mine, rows, 0.0), axis=0, keepdims=True)
    for r in range(RB):
        block_ref[r : r + 1, :MAIN] = own[:, r * MAIN : (r + 1) * MAIN]
        block_ref[r : r + 1, MAIN:] = own[:, SPLIT + r * REST : SPLIT + (r + 1) * REST]


def clip_kernel(square_ref, block_ref, out_ref):
    square = jnp.sum(jnp.sum(square_ref[...], axis=0), keepdims=True)
    factor = jnp.minimum(1.0, math.sqrt(D * E) * lax.rsqrt(square))
    out_ref[...] = block_ref[...] * factor


def call(kernel, inputs, outputs, flops, size, name, spaces=(), scratch=()):
    specs = [SMEM if value.ndim == 1 else VMEM for value in inputs]
    for i in spaces:
        specs[i] = pl.BlockSpec(memory_space=pl.ANY)
    return pl.pallas_call(
        kernel,
        out_shape=[jax.ShapeDtypeStruct(shape, dtype) for shape, dtype in outputs],
        in_specs=specs,
        out_specs=[VMEM] * len(outputs),
        scratch_shapes=list(scratch),
        compiler_params=pltpu.CompilerParams(vmem_limit_bytes=size << 20),
        cost_estimate=pl.CostEstimate(flops=flops, bytes_accessed=4 << 20, transcendentals=0),
        name=name,
    )(*inputs)


def traded(value, axis):
    return lax.all_to_all(value, axis, split_axis=0, concat_axis=0)


def total(value):
    return jnp.sum(value.astype(F32), axis=0)


def local(image_embeds, text_features, projection, pair_step, pair_col):
    x = lax.axis_index("x")
    places = (RIGHT_AT, RIGHT2_AT, LEFT2_AT, ACROSS_AT)
    place = [lax.axis_index(DP)] + [position_of(x, at) for at in places]
    place = jnp.stack(place + [lax.axis_index("c"), lax.axis_index(("zh", "z1"))]).astype(jnp.int32)
    image = image_embeds[0]
    features = text_features[0]
    right = shifted(image, RIGHT)
    left = shifted(image, LEFT)
    right2 = shifted(right, RIGHT2)
    left2 = shifted(left, LEFT2)
    across = shifted(right, ACROSS)

    full = (ROWS, E)
    table = (8, ROWS)
    unit, inverse, texts, acc, steps, cols = call(
        first_kernel,
        (place, features, projection, image, pair_step, pair_col),
        ((full, F32), ((ROWS, 128), F32), (full, BF16), (full, F32), (table, jnp.int32), (table, jnp.int32)),
        1 << 30, 48, "hidden_and_own", range(1, 6),
        (
            pltpu.VMEM((ROWS, D), BF16), pltpu.VMEM((D, E), BF16), pltpu.VMEM(full, BF16),
            pltpu.VMEM(pair_step.shape, jnp.int32), pltpu.VMEM(pair_col.shape, jnp.int32), pltpu.SemaphoreType.DMA((5,)),
        ),
    )
    turned, pick_there, pick_here = call(
        order_kernel, (place, features), (((D, ROWS), BF16), ((E, PICK), BF16), ((E, PICK), BF16)), 1 << 30, 32, "order"
    )
    swap = [(0, 1), (1, 0)]
    opposite = lax.ppermute(turned, "c", swap)
    (acc,) = call(near_kernel, (place, right, left, steps, cols, texts, acc), ((full, F32),), 1 << 30, 24, "near_pairs")
    for at, block, name in ((4, across, "far_across"), (2, right2, "far_right")):
        (acc,) = call(
            functools.partial(far_kernel, at), (place, block, steps, cols, texts, acc), ((full, F32),), 1 << 28, 24, name
        )
    grad, columns = call(
        last_kernel,
        (place, left2, steps, cols, texts, acc, unit, inverse, pick_there),
        ((full, BF16), ((ROWS, PICK), BF16)),
        1 << 30, 32, "far_left",
    )
    columns = lax.ppermute(columns, "c", swap)
    own, grad_text = call(
        own_kernel, (grad, pick_here, projection), (((ROWS, PICK), BF16), (full, BF16)), 1 << 28, 24, "own_columns"
    )
    (both,) = call(
        partial_kernel, (own, columns, turned, opposite), (((2, 2, SHARDS // 2, WIDTH), BF16),), 1 << 30, 32, "partial"
    )
    rows = total(traded(both.reshape(32, 8, WIDTH), NEAR)).astype(BF16)
    near = lax.ppermute(rows, "z1", swap)
    rows = (rows.astype(F32) + near.astype(F32)).astype(BF16)
    rows = traded(jnp.broadcast_to(rows[None], (4, 8, WIDTH)), "zh")
    block, square = call(block_kernel, (place, rows), (((RB, CB), F32), ((64, 8, 128), F32)), 1 << 20, 16, "block")
    square = traded(square, NEAR + ("c",))
    (block,) = call(clip_kernel, (square, block), (((RB, CB), F32),), 1 << 20, 16, "clip")
    return (grad_text[None], block)


def solution(mesh):
    split = Mesh(mesh.devices.reshape(SHAPE), AXES)
    placed = (
        P(OUTER, DP, None),
        P(OUTER, DP, None),
        P(),
        P(OUTER, None),
        P(OUTER, None),
    )
    return jax.shard_map(
        local,
        mesh=split,
        in_specs=placed,
        out_specs=(P(OUTER, DP, None), P(DP, OUTER)),
        check_vma=False,
    )
```

```python
import functools
import math

import jax
import jax.numpy as jnp
from jax import lax
from jax.experimental import pallas as pl
from jax.experimental.pallas import tpu as pltpu
from jax.sharding import Mesh, PartitionSpec as P

LOGIT_SCALE = 10.0
LOGIT_BIAS = -3.0
LOSS_SCALE = 256.0
EPSILON = 1e-06

SHARDS = 128
ROWS = 256
D = 1152
E = 1152
SHAPE = (2, 4, 2, 2, 4, 2, 2)
AXES = ("yh", "zh", "z1", "z0", "x", "yl", "c")
DP = ("yh", "zh", "z1", "z0", "x")
OUTER = ("yl", "c")
NEAR = ("yh", "yl", "x", "z0")
RB = 9
CB = 288
MAIN = 256
REST = 32
SPLIT = RB * MAIN
WIDTH = 2688
PICK = 2 * MAIN + 2 * 128

F32 = jnp.float32
BF16 = jnp.bfloat16
VMEM = pl.BlockSpec(memory_space=pltpu.VMEM)
SMEM = pl.BlockSpec(memory_space=pltpu.SMEM)


RIGHT = (1, 1, 1, -3)
LEFT = (-1, -1, -1, -1)
RIGHT2 = (1, 1, 1, 1)
LEFT2 = (-1, -1, 3, -1)
ACROSS = (4, -4, -4, -4)
RIGHT_AT = (5, 1, 1, 1)
LEFT_AT = (3, 3, 3, 3)
RIGHT2_AT = (0, 4, 0, 0)
LEFT2_AT = (4, 0, 4, 4)
ACROSS_AT = (1, 5, 5, 5)


def shifted(value, hops):
    pairs = [(source, (source + hops[source % 4]) % SHARDS) for source in range(SHARDS)]
    return lax.ppermute(value, DP, pairs)


def position_of(x, places):
    return jnp.where(x == 0, places[0], jnp.where(x == 1, places[1], jnp.where(x == 2, places[2], places[3])))


def dot(a, b):
    return jnp.dot(a, b, preferred_element_type=F32)


def dot_t(a, b):
    return lax.dot_general(a, b, (((1,), (1,)), ((), ())), preferred_element_type=F32)


def unit_rows(values):
    values = values.astype(F32)
    inverse = lax.rsqrt(jnp.sum(values * values, axis=-1, keepdims=True) + EPSILON)
    return values * inverse, inverse


def pair_grad(step_ref, col_ref, texts, block, position):
    images = unit_rows(block)[0].astype(BF16)
    steps = step_ref[pl.ds(position, 1), :]
    cols = col_ref[pl.ds(position, 1), :]
    logits = LOGIT_SCALE * dot_t(texts, images) + LOGIT_BIAS
    rows = lax.broadcasted_iota(jnp.int32, logits.shape, 0)
    positive = (steps == position) & (cols == rows)
    scale = LOSS_SCALE * LOGIT_SCALE
    chance = 1.0 / (1.0 + jnp.exp(jnp.where(positive, logits, -logits)))
    weights = (jnp.where(positive, -scale, scale) * chance).astype(BF16)
    return dot(weights, images)


def first_kernel(
    place_ref, feat_hbm, proj_hbm, image_hbm, step_hbm, col_hbm, unit_ref, inv_ref, text_ref, acc_ref, steps_ref, cols_ref,
    feat_ref, proj_ref, image_ref, step_ref, col_ref, sems,
):
    pairs = (
        (feat_hbm, feat_ref), (proj_hbm, proj_ref), (image_hbm, image_ref), (step_hbm, step_ref), (col_hbm, col_ref)
    )
    copies = [pltpu.make_async_copy(src, dst, sems.at[i]) for i, (src, dst) in enumerate(pairs)]
    for copy in copies:
        copy.start()
    copies[0].wait()
    copies[1].wait()
    hidden = dot(feat_ref[...], proj_ref[...])
    unit, inverse = unit_rows(hidden)
    texts = unit.astype(BF16)
    unit_ref[...] = unit
    inv_ref[...] = jnp.broadcast_to(inverse, inv_ref.shape)
    text_ref[...] = texts
    for copy in copies[2:]:
        copy.wait()
    for position in range(8):
        shard = (place_ref[0] + (position + (SHARDS - 2))) & (SHARDS - 1)
        spot = pl.ds(pl.multiple_of(shard * ROWS, ROWS), ROWS)
        steps_ref[position : position + 1, :] = step_ref[:, spot]
        cols_ref[position : position + 1, :] = col_ref[:, spot]
    acc_ref[...] = pair_grad(steps_ref, cols_ref, texts, image_ref[...], 2)


def near_kernel(place_ref, right_ref, left_ref, step_ref, col_ref, text_ref, acc_ref, out_ref):
    texts = text_ref[...]
    total = acc_ref[...] + pair_grad(step_ref, col_ref, texts, right_ref[...], place_ref[1])
    out_ref[...] = total + pair_grad(step_ref, col_ref, texts, left_ref[...], 3)


def column_of(lane, core):
    tail = lane - 2 * MAIN
    pair = jnp.where(lane < 2 * MAIN, lane >> 8, tail >> 7)
    inside = jnp.where(lane < 2 * MAIN, lane & (MAIN - 1), MAIN + (lane & (REST - 1)))
    return CB * (2 * pair + core) + inside


def order_kernel(place_ref, feat_ref, turned_ref, there_ref, here_ref):
    spot = lax.broadcasted_iota(jnp.int32, (D, 1), 0)
    within, peer = spot >> 7, spot & (SHARDS - 1)
    yh, x, z0, z = peer >> 6, (peer >> 4) & 3, (peer >> 3) & 1, peer & 7
    source = RB * (64 * yh + 8 * z + 4 * z0 + x) + within
    lanes = lax.broadcasted_iota(jnp.int32, (D, D), 1)
    order = jnp.where(lanes == source, 1.0, 0.0).astype(BF16)
    turned_ref[...] = dot_t(order, feat_ref[...]).astype(BF16)
    core = place_ref[5]
    lane = lax.broadcasted_iota(jnp.int32, (1, PICK), 1)
    rows = lax.broadcasted_iota(jnp.int32, (E, PICK), 0)
    there_ref[...] = jnp.where(rows == column_of(lane, 1 - core), 1.0, 0.0).astype(BF16)
    here_ref[...] = jnp.where(rows == column_of(lane, core), 1.0, 0.0).astype(BF16)


def far_kernel(at, place_ref, image_ref, step_ref, col_ref, text_ref, acc_ref, out_ref):
    part = pair_grad(step_ref, col_ref, text_ref[...], image_ref[...], place_ref[at])
    out_ref[...] = acc_ref[...] + part


def last_kernel(
    place_ref, left_ref, step_ref, col_ref, text_ref, acc_ref, unit_ref, inv_ref, pick_ref, grad_ref, out_ref
):
    part = pair_grad(step_ref, col_ref, text_ref[...], left_ref[...], place_ref[3])
    total = acc_ref[...] + part
    unit = unit_ref[...]
    radial = jnp.sum(unit * total, axis=-1, keepdims=True)
    grad = (inv_ref[:, :1] * (total - unit * radial)).astype(BF16)
    grad_ref[...] = grad
    out_ref[...] = dot(grad, pick_ref[...]).astype(BF16)


def own_kernel(grad_ref, pick_ref, proj_ref, out_ref, text_ref):
    out_ref[...] = dot(grad_ref[...], pick_ref[...]).astype(BF16)
    text_ref[...] = dot_t(grad_ref[...], proj_ref[...]).astype(BF16)


def partial_kernel(own_ref, came_ref, turned_ref, opposite_ref, out_ref):
    half = SHARDS // 2
    group = lax.broadcasted_iota(jnp.int32, (SHARDS, 128), 1) // REST
    rest = [[jnp.zeros((SHARDS, 128), F32) for _ in range(3)] for _ in range(2)]

    def put(pair, lanes, value):
        value = value.astype(BF16)
        for yh in range(2):
            out_ref[yh, pair, :, lanes] = value[yh * half : (yh + 1) * half]

    for r in range(RB):
        rows = slice(r * SHARDS, (r + 1) * SHARDS)
        block = dot(turned_ref[rows, :], own_ref[...]) + dot(opposite_ref[rows, :], came_ref[...])
        for pair in range(2):
            put(pair, slice(r * MAIN, (r + 1) * MAIN), block[:, pair * MAIN : (pair + 1) * MAIN])
            tail = block[:, 2 * MAIN + pair * 128 : 2 * MAIN + (pair + 1) * 128]
            rest[pair][r // 4] = jnp.where(group == r % 4, tail, rest[pair][r // 4])
    for pair in range(2):
        for t in range(3):
            put(pair, slice(SPLIT + t * 128, SPLIT + (t + 1) * 128), rest[pair][t])


def block_kernel(place_ref, came_ref, block_ref, square_ref):
    rows = jnp.sum(came_ref[...].astype(F32), axis=0)
    sums = jnp.sum(rows * rows, axis=0, keepdims=True)
    square = functools.reduce(jnp.add, [sums[:, t * 128 : (t + 1) * 128] for t in range(WIDTH // 128)])
    lines = lax.broadcasted_iota(jnp.int32, (8, 128), 0)
    square = jnp.where(lines == 0, jnp.broadcast_to(square, (8, 128)), 0.0)
    square_ref[...] = jnp.broadcast_to(square[None], square_ref.shape)
    mine = lax.broadcasted_iota(jnp.int32, rows.shape, 0) == place_ref[6]
    own = jnp.sum(jnp.where(mine, rows, 0.0), axis=0, keepdims=True)
    for r in range(RB):
        block_ref[r : r + 1, :MAIN] = own[:, r * MAIN : (r + 1) * MAIN]
        block_ref[r : r + 1, MAIN:] = own[:, SPLIT + r * REST : SPLIT + (r + 1) * REST]


def clip_kernel(square_ref, block_ref, out_ref):
    square = jnp.sum(jnp.sum(square_ref[...], axis=0), keepdims=True)
    factor = jnp.minimum(1.0, math.sqrt(D * E) * lax.rsqrt(square))
    out_ref[...] = block_ref[...] * factor


def call(kernel, inputs, outputs, flops, size, name, spaces=(), scratch=()):
    specs = [SMEM if value.ndim == 1 else VMEM for value in inputs]
    for i in spaces:
        specs[i] = pl.BlockSpec(memory_space=pl.ANY)
    return pl.pallas_call(
        kernel,
        out_shape=[jax.ShapeDtypeStruct(shape, dtype) for shape, dtype in outputs],
        in_specs=specs,
        out_specs=[VMEM] * len(outputs),
        scratch_shapes=list(scratch),
        compiler_params=pltpu.CompilerParams(vmem_limit_bytes=size << 20),
        cost_estimate=pl.CostEstimate(flops=flops, bytes_accessed=4 << 20, transcendentals=0),
        name=name,
    )(*inputs)


def traded(value, axis):
    return lax.all_to_all(value, axis, split_axis=0, concat_axis=0)


def total(value):
    return jnp.sum(value.astype(F32), axis=0)


def local(image_embeds, text_features, projection, pair_step, pair_col):
    x = lax.axis_index("x")
    places = (RIGHT_AT, RIGHT2_AT, LEFT2_AT, ACROSS_AT)
    place = [lax.axis_index(DP)] + [position_of(x, at) for at in places]
    place = jnp.stack(place + [lax.axis_index("c"), lax.axis_index(("zh", "z1"))]).astype(jnp.int32)
    image = image_embeds[0]
    features = text_features[0]
    right = shifted(image, RIGHT)
    left = shifted(image, LEFT)

    full = (ROWS, E)
    table = (8, ROWS)
    unit, inverse, texts, acc, steps, cols = call(
        first_kernel,
        (place, features, projection, image, pair_step, pair_col),
        ((full, F32), ((ROWS, 128), F32), (full, BF16), (full, F32), (table, jnp.int32), (table, jnp.int32)),
        1 << 30, 48, "hidden_and_own", range(1, 6),
        (
            pltpu.VMEM((ROWS, D), BF16), pltpu.VMEM((D, E), BF16), pltpu.VMEM(full, BF16),
            pltpu.VMEM(pair_step.shape, jnp.int32), pltpu.VMEM(pair_col.shape, jnp.int32), pltpu.SemaphoreType.DMA((5,)),
        ),
    )
    right, acc = lax.optimization_barrier((right, acc))
    right2 = shifted(right, RIGHT2)
    left2 = shifted(left, LEFT2)
    across = shifted(right, ACROSS)
    turned, pick_there, pick_here = call(
        order_kernel, (place, features), (((D, ROWS), BF16), ((E, PICK), BF16), ((E, PICK), BF16)), 1 << 30, 32, "order"
    )
    swap = [(0, 1), (1, 0)]
    opposite = lax.ppermute(turned, "c", swap)
    (acc,) = call(near_kernel, (place, right, left, steps, cols, texts, acc), ((full, F32),), 1 << 30, 24, "near_pairs")
    for at, block, name in ((4, across, "far_across"), (2, right2, "far_right")):
        (acc,) = call(
            functools.partial(far_kernel, at), (place, block, steps, cols, texts, acc), ((full, F32),), 1 << 28, 24, name
        )
    grad, columns = call(
        last_kernel,
        (place, left2, steps, cols, texts, acc, unit, inverse, pick_there),
        ((full, BF16), ((ROWS, PICK), BF16)),
        1 << 30, 32, "far_left",
    )
    columns = lax.ppermute(columns, "c", swap)
    own, grad_text = call(
        own_kernel, (grad, pick_here, projection), (((ROWS, PICK), BF16), (full, BF16)), 1 << 28, 24, "own_columns"
    )
    (both,) = call(
        partial_kernel, (own, columns, turned, opposite), (((2, 2, SHARDS // 2, WIDTH), BF16),), 1 << 30, 32, "partial"
    )
    rows = total(traded(both.reshape(32, 8, WIDTH), NEAR)).astype(BF16)
    near = lax.ppermute(rows, "z1", swap)
    rows = (rows.astype(F32) + near.astype(F32)).astype(BF16)
    rows = traded(jnp.broadcast_to(rows[None], (4, 8, WIDTH)), "zh")
    block, square = call(block_kernel, (place, rows), (((RB, CB), F32), ((64, 8, 128), F32)), 1 << 20, 16, "block")
    square = traded(square, NEAR + ("c",))
    (block,) = call(clip_kernel, (square, block), (((RB, CB), F32),), 1 << 20, 16, "clip")
    return (grad_text[None], block)


def solution(mesh):
    split = Mesh(mesh.devices.reshape(SHAPE), AXES)
    placed = (
        P(OUTER, DP, None),
        P(OUTER, DP, None),
        P(),
        P(OUTER, None),
        P(OUTER, None),
    )
    return jax.shard_map(
        local,
        mesh=split,
        in_specs=placed,
        out_specs=(P(OUTER, DP, None), P(DP, OUTER)),
        check_vma=False,
    )
```

```python
import functools
import math

import jax
import jax.numpy as jnp
from jax import lax
from jax.experimental import pallas as pl
from jax.experimental.pallas import tpu as pltpu
from jax.sharding import Mesh, PartitionSpec as P

LOGIT_SCALE = 10.0
LOGIT_BIAS = -3.0
LOSS_SCALE = 256.0
EPSILON = 1e-06

SHARDS = 128
ROWS = 256
D = 1152
E = 1152
SHAPE = (2, 4, 2, 2, 4, 2, 2)
AXES = ("yh", "zh", "z1", "z0", "x", "yl", "c")
DP = ("yh", "zh", "z1", "z0", "x")
OUTER = ("yl", "c")
NEAR = ("yh", "yl", "x", "z0")
RB = 9
CB = 288
MAIN = 256
REST = 32
SPLIT = RB * MAIN
WIDTH = 2688
PICK = 2 * MAIN + 2 * 128

F32 = jnp.float32
BF16 = jnp.bfloat16
VMEM = pl.BlockSpec(memory_space=pltpu.VMEM)
SMEM = pl.BlockSpec(memory_space=pltpu.SMEM)


RIGHT = (1, 1, 1, -3)
LEFT = (-1, -1, -1, -1)
RIGHT2 = (1, 1, 1, 1)
LEFT2 = (-1, -1, 3, -1)
ACROSS = (4, -4, -4, -4)
RIGHT_AT = (5, 1, 1, 1)
LEFT_AT = (3, 3, 3, 3)
RIGHT2_AT = (0, 4, 0, 0)
LEFT2_AT = (4, 0, 4, 4)
ACROSS_AT = (1, 5, 5, 5)


def shifted(value, hops):
    pairs = [(source, (source + hops[source % 4]) % SHARDS) for source in range(SHARDS)]
    return lax.ppermute(value, DP, pairs)


def position_of(x, places):
    return jnp.where(x == 0, places[0], jnp.where(x == 1, places[1], jnp.where(x == 2, places[2], places[3])))


def dot(a, b):
    return jnp.dot(a, b, preferred_element_type=F32)


def dot_t(a, b):
    return lax.dot_general(a, b, (((1,), (1,)), ((), ())), preferred_element_type=F32)


def unit_rows(values):
    values = values.astype(F32)
    inverse = lax.rsqrt(jnp.sum(values * values, axis=-1, keepdims=True) + EPSILON)
    return values * inverse, inverse


def pair_grad(step_ref, col_ref, texts, block, position):
    images = unit_rows(block)[0].astype(BF16)
    steps = step_ref[pl.ds(position, 1), :]
    cols = col_ref[pl.ds(position, 1), :]
    logits = LOGIT_SCALE * dot_t(texts, images) + LOGIT_BIAS
    rows = lax.broadcasted_iota(jnp.int32, logits.shape, 0)
    positive = (steps == position) & (cols == rows)
    scale = LOSS_SCALE * LOGIT_SCALE
    chance = 1.0 / (1.0 + jnp.exp(jnp.where(positive, logits, -logits)))
    weights = (jnp.where(positive, -scale, scale) * chance).astype(BF16)
    return dot(weights, images)


def first_kernel(
    place_ref, feat_hbm, proj_hbm, image_hbm, step_hbm, col_hbm, unit_ref, inv_ref, text_ref, acc_ref, steps_ref, cols_ref,
    feat_ref, proj_ref, image_ref, step_ref, col_ref, sems,
):
    pairs = (
        (feat_hbm, feat_ref), (proj_hbm, proj_ref), (image_hbm, image_ref), (step_hbm, step_ref), (col_hbm, col_ref)
    )
    copies = [pltpu.make_async_copy(src, dst, sems.at[i]) for i, (src, dst) in enumerate(pairs)]
    for copy in copies:
        copy.start()
    copies[0].wait()
    copies[1].wait()
    hidden = dot(feat_ref[...], proj_ref[...])
    unit, inverse = unit_rows(hidden)
    texts = unit.astype(BF16)
    unit_ref[...] = unit
    inv_ref[...] = jnp.broadcast_to(inverse, inv_ref.shape)
    text_ref[...] = texts
    for copy in copies[2:]:
        copy.wait()
    for position in range(8):
        shard = (place_ref[0] + (position + (SHARDS - 2))) & (SHARDS - 1)
        spot = pl.ds(pl.multiple_of(shard * ROWS, ROWS), ROWS)
        steps_ref[position : position + 1, :] = step_ref[:, spot]
        cols_ref[position : position + 1, :] = col_ref[:, spot]
    acc_ref[...] = pair_grad(steps_ref, cols_ref, texts, image_ref[...], 2)


def near_kernel(place_ref, right_ref, left_ref, step_ref, col_ref, text_ref, acc_ref, out_ref):
    texts = text_ref[...]
    total = acc_ref[...] + pair_grad(step_ref, col_ref, texts, right_ref[...], place_ref[1])
    out_ref[...] = total + pair_grad(step_ref, col_ref, texts, left_ref[...], 3)


def column_of(lane, core):
    tail = lane - 2 * MAIN
    pair = jnp.where(lane < 2 * MAIN, lane >> 8, tail >> 7)
    inside = jnp.where(lane < 2 * MAIN, lane & (MAIN - 1), MAIN + (lane & (REST - 1)))
    return CB * (2 * pair + core) + inside


def order_kernel(place_ref, feat_ref, turned_ref, there_ref, here_ref):
    spot = lax.broadcasted_iota(jnp.int32, (D, 1), 0)
    within, peer = spot >> 7, spot & (SHARDS - 1)
    yh, x, z0, z = peer >> 6, (peer >> 4) & 3, (peer >> 3) & 1, peer & 7
    source = RB * (64 * yh + 8 * z + 4 * z0 + x) + within
    lanes = lax.broadcasted_iota(jnp.int32, (D, D), 1)
    order = jnp.where(lanes == source, 1.0, 0.0).astype(BF16)
    turned_ref[...] = dot_t(order, feat_ref[...]).astype(BF16)
    core = place_ref[5]
    lane = lax.broadcasted_iota(jnp.int32, (1, PICK), 1)
    rows = lax.broadcasted_iota(jnp.int32, (E, PICK), 0)
    there_ref[...] = jnp.where(rows == column_of(lane, 1 - core), 1.0, 0.0).astype(BF16)
    here_ref[...] = jnp.where(rows == column_of(lane, core), 1.0, 0.0).astype(BF16)


def far_kernel(at, place_ref, image_ref, step_ref, col_ref, text_ref, acc_ref, out_ref):
    part = pair_grad(step_ref, col_ref, text_ref[...], image_ref[...], place_ref[at])
    out_ref[...] = acc_ref[...] + part


def last_kernel(
    place_ref, left_ref, step_ref, col_ref, text_ref, acc_ref, unit_ref, inv_ref, pick_ref, grad_ref, out_ref
):
    part = pair_grad(step_ref, col_ref, text_ref[...], left_ref[...], place_ref[3])
    total = acc_ref[...] + part
    unit = unit_ref[...]
    radial = jnp.sum(unit * total, axis=-1, keepdims=True)
    grad = (inv_ref[:, :1] * (total - unit * radial)).astype(BF16)
    grad_ref[...] = grad
    out_ref[...] = dot(grad, pick_ref[...]).astype(BF16)


def own_kernel(grad_ref, pick_ref, proj_ref, out_ref, text_ref):
    out_ref[...] = dot(grad_ref[...], pick_ref[...]).astype(BF16)
    text_ref[...] = dot_t(grad_ref[...], proj_ref[...]).astype(BF16)


def partial_kernel(own_ref, came_ref, turned_ref, opposite_ref, out_ref):
    half = SHARDS // 2
    group = lax.broadcasted_iota(jnp.int32, (SHARDS, 128), 1) // REST
    rest = [[jnp.zeros((SHARDS, 128), F32) for _ in range(3)] for _ in range(2)]

    def put(pair, lanes, value):
        value = value.astype(BF16)
        for yh in range(2):
            out_ref[yh, pair, :, lanes] = value[yh * half : (yh + 1) * half]

    for r in range(RB):
        rows = slice(r * SHARDS, (r + 1) * SHARDS)
        block = dot(turned_ref[rows, :], own_ref[...]) + dot(opposite_ref[rows, :], came_ref[...])
        for pair in range(2):
            put(pair, slice(r * MAIN, (r + 1) * MAIN), block[:, pair * MAIN : (pair + 1) * MAIN])
            tail = block[:, 2 * MAIN + pair * 128 : 2 * MAIN + (pair + 1) * 128]
            rest[pair][r // 4] = jnp.where(group == r % 4, tail, rest[pair][r // 4])
    for pair in range(2):
        for t in range(3):
            put(pair, slice(SPLIT + t * 128, SPLIT + (t + 1) * 128), rest[pair][t])


def block_kernel(place_ref, came_ref, block_ref, square_ref):
    rows = jnp.sum(came_ref[...].astype(F32), axis=0)
    sums = jnp.sum(rows * rows, axis=0, keepdims=True)
    square = functools.reduce(jnp.add, [sums[:, t * 128 : (t + 1) * 128] for t in range(WIDTH // 128)])
    lines = lax.broadcasted_iota(jnp.int32, (8, 128), 0)
    square = jnp.where(lines == 0, jnp.broadcast_to(square, (8, 128)), 0.0)
    square_ref[...] = jnp.broadcast_to(square[None], square_ref.shape)
    mine = lax.broadcasted_iota(jnp.int32, rows.shape, 0) == place_ref[6]
    own = jnp.sum(jnp.where(mine, rows, 0.0), axis=0, keepdims=True)
    for r in range(RB):
        block_ref[r : r + 1, :MAIN] = own[:, r * MAIN : (r + 1) * MAIN]
        block_ref[r : r + 1, MAIN:] = own[:, SPLIT + r * REST : SPLIT + (r + 1) * REST]


def clip_kernel(square_ref, block_ref, out_ref):
    square = jnp.sum(jnp.sum(square_ref[...], axis=0), keepdims=True)
    factor = jnp.minimum(1.0, math.sqrt(D * E) * lax.rsqrt(square))
    out_ref[...] = block_ref[...] * factor


def call(kernel, inputs, outputs, flops, size, name, spaces=(), scratch=()):
    specs = [SMEM if value.ndim == 1 else VMEM for value in inputs]
    for i in spaces:
        specs[i] = pl.BlockSpec(memory_space=pl.ANY)
    return pl.pallas_call(
        kernel,
        out_shape=[jax.ShapeDtypeStruct(shape, dtype) for shape, dtype in outputs],
        in_specs=specs,
        out_specs=[VMEM] * len(outputs),
        scratch_shapes=list(scratch),
        compiler_params=pltpu.CompilerParams(vmem_limit_bytes=size << 20),
        cost_estimate=pl.CostEstimate(flops=flops, bytes_accessed=4 << 20, transcendentals=0),
        name=name,
    )(*inputs)


def traded(value, axis):
    return lax.all_to_all(value, axis, split_axis=0, concat_axis=0)


def total(value):
    return jnp.sum(value.astype(F32), axis=0)


def local(image_embeds, text_features, projection, pair_step, pair_col):
    x = lax.axis_index("x")
    places = (RIGHT_AT, RIGHT2_AT, LEFT2_AT, ACROSS_AT)
    place = [lax.axis_index(DP)] + [position_of(x, at) for at in places]
    place = jnp.stack(place + [lax.axis_index("c"), lax.axis_index(("zh", "z1"))]).astype(jnp.int32)
    image = image_embeds[0]
    features = text_features[0]
    right = shifted(image, RIGHT)
    left = shifted(image, LEFT)
    right2 = shifted(right, RIGHT2)
    left2 = shifted(left, LEFT2)
    across = shifted(right, ACROSS)

    full = (ROWS, E)
    table = (8, ROWS)
    unit, inverse, texts, acc, steps, cols = call(
        first_kernel,
        (place, features, projection, image, pair_step, pair_col),
        ((full, F32), ((ROWS, 128), F32), (full, BF16), (full, F32), (table, jnp.int32), (table, jnp.int32)),
        1 << 30, 48, "hidden_and_own", range(1, 6),
        (
            pltpu.VMEM((ROWS, D), BF16), pltpu.VMEM((D, E), BF16), pltpu.VMEM(full, BF16),
            pltpu.VMEM(pair_step.shape, jnp.int32), pltpu.VMEM(pair_col.shape, jnp.int32), pltpu.SemaphoreType.DMA((5,)),
        ),
    )
    turned, pick_there, pick_here = call(
        order_kernel, (place, features), (((D, ROWS), BF16), ((E, PICK), BF16), ((E, PICK), BF16)), 1 << 30, 32, "order"
    )
    swap = [(0, 1), (1, 0)]
    opposite = lax.ppermute(turned, "c", swap)
    (acc,) = call(near_kernel, (place, right, left, steps, cols, texts, acc), ((full, F32),), 1 << 30, 24, "near_pairs")
    for at, block, name in ((4, across, "far_across"), (2, right2, "far_right")):
        (acc,) = call(
            functools.partial(far_kernel, at), (place, block, steps, cols, texts, acc), ((full, F32),), 1 << 28, 24, name
        )
    grad, columns = call(
        last_kernel,
        (place, left2, steps, cols, texts, acc, unit, inverse, pick_there),
        ((full, BF16), ((ROWS, PICK), BF16)),
        1 << 30, 32, "far_left",
    )
    columns = lax.ppermute(columns, "c", swap)
    own, grad_text = call(
        own_kernel, (grad, pick_here, projection), (((ROWS, PICK), BF16), (full, BF16)), 1 << 28, 24, "own_columns"
    )
    (both,) = call(
        partial_kernel, (own, columns, turned, opposite), (((2, 2, SHARDS // 2, WIDTH), BF16),), 1 << 30, 32, "partial"
    )
    rows = total(traded(both.reshape(32, 8, WIDTH), NEAR)).astype(BF16)
    rows = traded(jnp.broadcast_to(rows[None], (8, 8, WIDTH)), ("zh", "z1"))
    block, square = call(block_kernel, (place, rows), (((RB, CB), F32), ((64, 8, 128), F32)), 1 << 20, 16, "block")
    square = traded(square, NEAR + ("c",))
    (block,) = call(clip_kernel, (square, block), (((RB, CB), F32),), 1 << 20, 16, "clip")
    return (grad_text[None], block)


def solution(mesh):
    split = Mesh(mesh.devices.reshape(SHAPE), AXES)
    placed = (
        P(OUTER, DP, None),
        P(OUTER, DP, None),
        P(),
        P(OUTER, None),
        P(OUTER, None),
    )
    return jax.shard_map(
        local,
        mesh=split,
        in_specs=placed,
        out_specs=(P(OUTER, DP, None), P(DP, OUTER)),
        check_vma=False,
    )
```

```python
import functools
import math

import jax
import jax.numpy as jnp
from jax import lax
from jax.experimental import pallas as pl
from jax.experimental.pallas import tpu as pltpu
from jax.sharding import Mesh, PartitionSpec as P

LOGIT_SCALE = 10.0
LOGIT_BIAS = -3.0
LOSS_SCALE = 256.0
EPSILON = 1e-06

SHARDS = 128
ROWS = 256
D = 1152
E = 1152
SHAPE = (2, 4, 2, 2, 4, 2, 2)
AXES = ("yh", "zh", "z1", "z0", "x", "yl", "c")
DP = ("yh", "zh", "z1", "z0", "x")
OUTER = ("yl", "c")
NEAR = ("yh", "yl", "x", "z0")
RB = 9
CB = 288
MAIN = 256
REST = 32
SPLIT = RB * MAIN
WIDTH = 2688
PICK = 2 * MAIN + 2 * 128

F32 = jnp.float32
BF16 = jnp.bfloat16
VMEM = pl.BlockSpec(memory_space=pltpu.VMEM)
SMEM = pl.BlockSpec(memory_space=pltpu.SMEM)


RIGHT = (1, 1, 1, -3)
LEFT = (-1, -1, -1, -1)
RIGHT2 = (1, 1, 1, 1)
LEFT2 = (-1, -1, 3, -1)
ACROSS = (4, -4, -4, -4)
RIGHT_AT = (5, 1, 1, 1)
LEFT_AT = (3, 3, 3, 3)
RIGHT2_AT = (0, 4, 0, 0)
LEFT2_AT = (4, 0, 4, 4)
ACROSS_AT = (1, 5, 5, 5)


def shifted(value, hops):
    pairs = [(source, (source + hops[source % 4]) % SHARDS) for source in range(SHARDS)]
    return lax.ppermute(value, DP, pairs)


def position_of(x, places):
    return jnp.where(x == 0, places[0], jnp.where(x == 1, places[1], jnp.where(x == 2, places[2], places[3])))


def dot(a, b):
    return jnp.dot(a, b, preferred_element_type=F32)


def dot_t(a, b):
    return lax.dot_general(a, b, (((1,), (1,)), ((), ())), preferred_element_type=F32)


def unit_rows(values):
    values = values.astype(F32)
    inverse = lax.rsqrt(jnp.sum(values * values, axis=-1, keepdims=True) + EPSILON)
    return values * inverse, inverse


def pair_grad(step_ref, col_ref, texts, block, position):
    images = unit_rows(block)[0].astype(BF16)
    steps = step_ref[pl.ds(position, 1), :]
    cols = col_ref[pl.ds(position, 1), :]
    logits = LOGIT_SCALE * dot_t(texts, images) + LOGIT_BIAS
    rows = lax.broadcasted_iota(jnp.int32, logits.shape, 0)
    positive = (steps == position) & (cols == rows)
    scale = LOSS_SCALE * LOGIT_SCALE
    chance = 1.0 / (1.0 + jnp.exp(jnp.where(positive, logits, -logits)))
    weights = (jnp.where(positive, -scale, scale) * chance).astype(BF16)
    return dot(weights, images)


def first_kernel(
    place_ref, feat_hbm, proj_hbm, image_hbm, step_hbm, col_hbm, unit_ref, inv_ref, text_ref, acc_ref, steps_ref, cols_ref,
    feat_ref, proj_ref, image_ref, step_ref, col_ref, sems,
):
    pairs = (
        (feat_hbm, feat_ref), (proj_hbm, proj_ref), (image_hbm, image_ref), (step_hbm, step_ref), (col_hbm, col_ref)
    )
    copies = [pltpu.make_async_copy(src, dst, sems.at[i]) for i, (src, dst) in enumerate(pairs)]
    for copy in copies:
        copy.start()
    copies[0].wait()
    copies[1].wait()
    hidden = dot(feat_ref[...], proj_ref[...])
    unit, inverse = unit_rows(hidden)
    texts = unit.astype(BF16)
    unit_ref[...] = unit
    inv_ref[...] = jnp.broadcast_to(inverse, inv_ref.shape)
    text_ref[...] = texts
    for copy in copies[2:]:
        copy.wait()
    for position in range(8):
        shard = (place_ref[0] + (position + (SHARDS - 2))) & (SHARDS - 1)
        spot = pl.ds(pl.multiple_of(shard * ROWS, ROWS), ROWS)
        steps_ref[position : position + 1, :] = step_ref[:, spot]
        cols_ref[position : position + 1, :] = col_ref[:, spot]
    acc_ref[...] = pair_grad(steps_ref, cols_ref, texts, image_ref[...], 2)


def near_kernel(place_ref, right_ref, left_ref, step_ref, col_ref, text_ref, acc_ref, out_ref):
    texts = text_ref[...]
    total = acc_ref[...] + pair_grad(step_ref, col_ref, texts, right_ref[...], place_ref[1])
    out_ref[...] = total + pair_grad(step_ref, col_ref, texts, left_ref[...], 3)


def column_of(lane, core):
    tail = lane - 2 * MAIN
    pair = jnp.where(lane < 2 * MAIN, lane >> 8, tail >> 7)
    inside = jnp.where(lane < 2 * MAIN, lane & (MAIN - 1), MAIN + (lane & (REST - 1)))
    return CB * (2 * pair + core) + inside


def order_kernel(place_ref, feat_ref, turned_ref, there_ref, here_ref):
    spot = lax.broadcasted_iota(jnp.int32, (D, 1), 0)
    within, peer = spot >> 7, spot & (SHARDS - 1)
    yh, x, z0, z = peer >> 6, (peer >> 4) & 3, (peer >> 3) & 1, peer & 7
    source = RB * (64 * yh + 8 * z + 4 * z0 + x) + within
    lanes = lax.broadcasted_iota(jnp.int32, (D, D), 1)
    order = jnp.where(lanes == source, 1.0, 0.0).astype(BF16)
    turned_ref[...] = dot_t(order, feat_ref[...]).astype(BF16)
    core = place_ref[5]
    lane = lax.broadcasted_iota(jnp.int32, (1, PICK), 1)
    rows = lax.broadcasted_iota(jnp.int32, (E, PICK), 0)
    there_ref[...] = jnp.where(rows == column_of(lane, 1 - core), 1.0, 0.0).astype(BF16)
    here_ref[...] = jnp.where(rows == column_of(lane, core), 1.0, 0.0).astype(BF16)


def far_kernel(at, place_ref, image_ref, step_ref, col_ref, text_ref, acc_ref, out_ref):
    part = pair_grad(step_ref, col_ref, text_ref[...], image_ref[...], place_ref[at])
    out_ref[...] = acc_ref[...] + part


def last_kernel(
    place_ref, left_ref, step_ref, col_ref, text_ref, acc_ref, unit_ref, inv_ref, pick_ref, grad_ref, out_ref
):
    part = pair_grad(step_ref, col_ref, text_ref[...], left_ref[...], place_ref[3])
    total = acc_ref[...] + part
    unit = unit_ref[...]
    radial = jnp.sum(unit * total, axis=-1, keepdims=True)
    grad = (inv_ref[:, :1] * (total - unit * radial)).astype(BF16)
    grad_ref[...] = grad
    out_ref[...] = dot(grad, pick_ref[...]).astype(BF16)


def own_kernel(grad_ref, pick_ref, proj_ref, out_ref, text_ref):
    out_ref[...] = dot(grad_ref[...], pick_ref[...]).astype(BF16)
    text_ref[...] = dot_t(grad_ref[...], proj_ref[...]).astype(BF16)


def partial_kernel(own_ref, came_ref, turned_ref, opposite_ref, out_ref):
    half = SHARDS // 2
    group = lax.broadcasted_iota(jnp.int32, (SHARDS, 128), 1) // REST
    rest = [[jnp.zeros((SHARDS, 128), F32) for _ in range(3)] for _ in range(2)]

    def put(pair, lanes, value):
        value = value.astype(BF16)
        for yh in range(2):
            out_ref[yh, pair, :, lanes] = value[yh * half : (yh + 1) * half]

    for r in range(RB):
        rows = slice(r * SHARDS, (r + 1) * SHARDS)
        block = dot(turned_ref[rows, :], own_ref[...]) + dot(opposite_ref[rows, :], came_ref[...])
        for pair in range(2):
            put(pair, slice(r * MAIN, (r + 1) * MAIN), block[:, pair * MAIN : (pair + 1) * MAIN])
            tail = block[:, 2 * MAIN + pair * 128 : 2 * MAIN + (pair + 1) * 128]
            rest[pair][r // 4] = jnp.where(group == r % 4, tail, rest[pair][r // 4])
    for pair in range(2):
        for t in range(3):
            put(pair, slice(SPLIT + t * 128, SPLIT + (t + 1) * 128), rest[pair][t])


def block_kernel(place_ref, came_ref, block_ref, square_ref):
    rows = jnp.sum(came_ref[...].astype(F32), axis=0)
    sums = jnp.sum(rows * rows, axis=0, keepdims=True)
    square = functools.reduce(jnp.add, [sums[:, t * 128 : (t + 1) * 128] for t in range(WIDTH // 128)])
    square_ref[...] = jnp.broadcast_to(square[None], square_ref.shape)
    mine = lax.broadcasted_iota(jnp.int32, rows.shape, 0) == place_ref[6]
    own = jnp.sum(jnp.where(mine, rows, 0.0), axis=0, keepdims=True)
    for r in range(RB):
        block_ref[r : r + 1, :MAIN] = own[:, r * MAIN : (r + 1) * MAIN]
        block_ref[r : r + 1, MAIN:] = own[:, SPLIT + r * REST : SPLIT + (r + 1) * REST]


def clip_kernel(square_ref, block_ref, out_ref):
    square = jnp.sum(jnp.sum(square_ref[...], axis=0), keepdims=True)
    factor = jnp.minimum(1.0, math.sqrt(D * E) * lax.rsqrt(square))
    out_ref[...] = block_ref[...] * factor


def call(kernel, inputs, outputs, flops, size, name, spaces=(), scratch=()):
    specs = [SMEM if value.ndim == 1 else VMEM for value in inputs]
    for i in spaces:
        specs[i] = pl.BlockSpec(memory_space=pl.ANY)
    return pl.pallas_call(
        kernel,
        out_shape=[jax.ShapeDtypeStruct(shape, dtype) for shape, dtype in outputs],
        in_specs=specs,
        out_specs=[VMEM] * len(outputs),
        scratch_shapes=list(scratch),
        compiler_params=pltpu.CompilerParams(vmem_limit_bytes=size << 20),
        cost_estimate=pl.CostEstimate(flops=flops, bytes_accessed=4 << 20, transcendentals=0),
        name=name,
    )(*inputs)


def traded(value, axis):
    return lax.all_to_all(value, axis, split_axis=0, concat_axis=0)


def total(value):
    return jnp.sum(value.astype(F32), axis=0)


def local(image_embeds, text_features, projection, pair_step, pair_col):
    x = lax.axis_index("x")
    places = (RIGHT_AT, RIGHT2_AT, LEFT2_AT, ACROSS_AT)
    place = [lax.axis_index(DP)] + [position_of(x, at) for at in places]
    place = jnp.stack(place + [lax.axis_index("c"), lax.axis_index(("zh", "z1"))]).astype(jnp.int32)
    image = image_embeds[0]
    features = text_features[0]
    right = shifted(image, RIGHT)
    left = shifted(image, LEFT)
    right2 = shifted(right, RIGHT2)
    left2 = shifted(left, LEFT2)
    across = shifted(right, ACROSS)

    full = (ROWS, E)
    table = (8, ROWS)
    unit, inverse, texts, acc, steps, cols = call(
        first_kernel,
        (place, features, projection, image, pair_step, pair_col),
        ((full, F32), ((ROWS, 128), F32), (full, BF16), (full, F32), (table, jnp.int32), (table, jnp.int32)),
        1 << 30, 48, "hidden_and_own", range(1, 6),
        (
            pltpu.VMEM((ROWS, D), BF16), pltpu.VMEM((D, E), BF16), pltpu.VMEM(full, BF16),
            pltpu.VMEM(pair_step.shape, jnp.int32), pltpu.VMEM(pair_col.shape, jnp.int32), pltpu.SemaphoreType.DMA((5,)),
        ),
    )
    turned, pick_there, pick_here = call(
        order_kernel, (place, features), (((D, ROWS), BF16), ((E, PICK), BF16), ((E, PICK), BF16)), 1 << 30, 32, "order"
    )
    swap = [(0, 1), (1, 0)]
    opposite = lax.ppermute(turned, "c", swap)
    (acc,) = call(near_kernel, (place, right, left, steps, cols, texts, acc), ((full, F32),), 1 << 30, 24, "near_pairs")
    for at, block, name in ((4, across, "far_across"), (2, right2, "far_right")):
        (acc,) = call(
            functools.partial(far_kernel, at), (place, block, steps, cols, texts, acc), ((full, F32),), 1 << 28, 24, name
        )
    grad, columns = call(
        last_kernel,
        (place, left2, steps, cols, texts, acc, unit, inverse, pick_there),
        ((full, BF16), ((ROWS, PICK), BF16)),
        1 << 30, 32, "far_left",
    )
    columns = lax.ppermute(columns, "c", swap)
    own, grad_text = call(
        own_kernel, (grad, pick_here, projection), (((ROWS, PICK), BF16), (full, BF16)), 1 << 28, 24, "own_columns"
    )
    (both,) = call(
        partial_kernel, (own, columns, turned, opposite), (((2, 2, SHARDS // 2, WIDTH), BF16),), 1 << 30, 32, "partial"
    )
    rows = total(traded(both.reshape(32, 8, WIDTH), NEAR)).astype(BF16)
    near = lax.ppermute(rows, "z1", swap)
    rows = (rows.astype(F32) + near.astype(F32)).astype(BF16)
    rows = traded(jnp.broadcast_to(rows[None], (4, 8, WIDTH)), "zh")
    block, square = call(block_kernel, (place, rows), (((RB, CB), F32), ((64, 1, 128), F32)), 1 << 20, 16, "block")
    square = traded(square, NEAR + ("c",))
    (block,) = call(clip_kernel, (square, block), (((RB, CB), F32),), 1 << 20, 16, "clip")
    return (grad_text[None], block)


def solution(mesh):
    split = Mesh(mesh.devices.reshape(SHAPE), AXES)
    placed = (
        P(OUTER, DP, None),
        P(OUTER, DP, None),
        P(),
        P(OUTER, None),
        P(OUTER, None),
    )
    return jax.shard_map(
        local,
        mesh=split,
        in_specs=placed,
        out_specs=(P(OUTER, DP, None), P(DP, OUTER)),
        check_vma=False,
    )
```

```python
import functools
import math

import jax
import jax.numpy as jnp
from jax import lax
from jax.experimental import pallas as pl
from jax.experimental.pallas import tpu as pltpu
from jax.sharding import Mesh, PartitionSpec as P

LOGIT_SCALE = 10.0
LOGIT_BIAS = -3.0
LOSS_SCALE = 256.0
EPSILON = 1e-06

SHARDS = 128
ROWS = 256
D = 1152
E = 1152
SHAPE = (2, 4, 2, 2, 4, 2, 2)
AXES = ("yh", "zh", "z1", "z0", "x", "yl", "c")
DP = ("yh", "zh", "z1", "z0", "x")
OUTER = ("yl", "c")
NEAR = ("yh", "yl", "x", "z0")
RB = 9
CB = 288
MAIN = 256
REST = 32
SPLIT = RB * MAIN
WIDTH = 2688
PICK = 2 * MAIN + 2 * 128

F32 = jnp.float32
BF16 = jnp.bfloat16
VMEM = pl.BlockSpec(memory_space=pltpu.VMEM)
SMEM = pl.BlockSpec(memory_space=pltpu.SMEM)


RIGHT = (1, 1, 1, -3)
LEFT = (-1, -1, -1, -1)
RIGHT2 = (1, 1, 1, 1)
LEFT2 = (-1, -1, 3, -1)
ACROSS = (4, -4, -4, -4)
RIGHT_AT = (5, 1, 1, 1)
LEFT_AT = (3, 3, 3, 3)
RIGHT2_AT = (0, 4, 0, 0)
LEFT2_AT = (4, 0, 4, 4)
ACROSS_AT = (1, 5, 5, 5)


def shifted(value, hops):
    pairs = [(source, (source + hops[source % 4]) % SHARDS) for source in range(SHARDS)]
    return lax.ppermute(value, DP, pairs)


def position_of(x, places):
    return jnp.where(x == 0, places[0], jnp.where(x == 1, places[1], jnp.where(x == 2, places[2], places[3])))


def dot(a, b):
    return jnp.dot(a, b, preferred_element_type=F32)


def dot_t(a, b):
    return lax.dot_general(a, b, (((1,), (1,)), ((), ())), preferred_element_type=F32)


def unit_rows(values):
    values = values.astype(F32)
    inverse = lax.rsqrt(jnp.sum(values * values, axis=-1, keepdims=True) + EPSILON)
    return values * inverse, inverse


def pair_grad(step_ref, col_ref, texts, block, position):
    images = unit_rows(block)[0].astype(BF16)
    steps = step_ref[pl.ds(position, 1), :]
    cols = col_ref[pl.ds(position, 1), :]
    logits = LOGIT_SCALE * dot_t(texts, images) + LOGIT_BIAS
    rows = lax.broadcasted_iota(jnp.int32, logits.shape, 0)
    positive = (steps == position) & (cols == rows)
    scale = LOSS_SCALE * LOGIT_SCALE
    chance = 1.0 / (1.0 + jnp.exp(jnp.where(positive, logits, -logits)))
    weights = (jnp.where(positive, -scale, scale) * chance).astype(BF16)
    return dot(weights, images)


def first_kernel(
    place_ref, feat_hbm, proj_hbm, image_hbm, step_hbm, col_hbm, unit_ref, inv_ref, text_ref, acc_ref, steps_ref, cols_ref,
    feat_ref, proj_ref, image_ref, step_ref, col_ref, sems,
):
    pairs = (
        (feat_hbm, feat_ref), (proj_hbm, proj_ref), (image_hbm, image_ref), (step_hbm, step_ref), (col_hbm, col_ref)
    )
    copies = [pltpu.make_async_copy(src, dst, sems.at[i]) for i, (src, dst) in enumerate(pairs)]
    for copy in copies:
        copy.start()
    copies[0].wait()
    copies[1].wait()
    hidden = dot(feat_ref[...], proj_ref[...])
    unit, inverse = unit_rows(hidden)
    texts = unit.astype(BF16)
    unit_ref[...] = unit
    inv_ref[...] = jnp.broadcast_to(inverse, inv_ref.shape)
    text_ref[...] = texts
    for copy in copies[2:]:
        copy.wait()
    for position in range(8):
        shard = (place_ref[0] + (position + (SHARDS - 2))) & (SHARDS - 1)
        spot = pl.ds(pl.multiple_of(shard * ROWS, ROWS), ROWS)
        steps_ref[position : position + 1, :] = step_ref[:, spot]
        cols_ref[position : position + 1, :] = col_ref[:, spot]
    acc_ref[...] = pair_grad(steps_ref, cols_ref, texts, image_ref[...], 2)


def near_kernel(place_ref, right_ref, left_ref, step_ref, col_ref, text_ref, acc_ref, out_ref):
    texts = text_ref[...]
    total = acc_ref[...] + pair_grad(step_ref, col_ref, texts, right_ref[...], place_ref[1])
    out_ref[...] = total + pair_grad(step_ref, col_ref, texts, left_ref[...], 3)


def column_of(lane, core):
    tail = lane - 2 * MAIN
    pair = jnp.where(lane < 2 * MAIN, lane >> 8, tail >> 7)
    inside = jnp.where(lane < 2 * MAIN, lane & (MAIN - 1), MAIN + (lane & (REST - 1)))
    return CB * (2 * pair + core) + inside


def order_kernel(place_ref, feat_ref, turned_ref, there_ref, here_ref):
    spot = lax.broadcasted_iota(jnp.int32, (D, 1), 0)
    within, peer = spot >> 7, spot & (SHARDS - 1)
    yh, x, z0, z = peer >> 6, (peer >> 4) & 3, (peer >> 3) & 1, peer & 7
    source = RB * (64 * yh + 8 * z + 4 * z0 + x) + within
    lanes = lax.broadcasted_iota(jnp.int32, (D, D), 1)
    order = jnp.where(lanes == source, 1.0, 0.0).astype(BF16)
    turned_ref[...] = dot_t(order, feat_ref[...]).astype(BF16)
    core = place_ref[5]
    lane = lax.broadcasted_iota(jnp.int32, (1, PICK), 1)
    rows = lax.broadcasted_iota(jnp.int32, (E, PICK), 0)
    there_ref[...] = jnp.where(rows == column_of(lane, 1 - core), 1.0, 0.0).astype(BF16)
    here_ref[...] = jnp.where(rows == column_of(lane, core), 1.0, 0.0).astype(BF16)


def far_kernel(at, place_ref, image_ref, step_ref, col_ref, text_ref, acc_ref, out_ref):
    part = pair_grad(step_ref, col_ref, text_ref[...], image_ref[...], place_ref[at])
    out_ref[...] = acc_ref[...] + part


def last_kernel(
    place_ref, left_ref, step_ref, col_ref, text_ref, acc_ref, unit_ref, inv_ref, pick_ref, grad_ref, out_ref
):
    part = pair_grad(step_ref, col_ref, text_ref[...], left_ref[...], place_ref[3])
    total = acc_ref[...] + part
    unit = unit_ref[...]
    radial = jnp.sum(unit * total, axis=-1, keepdims=True)
    grad = (inv_ref[:, :1] * (total - unit * radial)).astype(BF16)
    grad_ref[...] = grad
    out_ref[...] = dot(grad, pick_ref[...]).astype(BF16)


def own_kernel(grad_ref, pick_ref, out_ref):
    out_ref[...] = dot(grad_ref[...], pick_ref[...]).astype(BF16)


def text_kernel(grad_ref, proj_ref, out_ref):
    out_ref[...] = dot_t(grad_ref[...], proj_ref[...]).astype(BF16)


def partial_kernel(own_ref, came_ref, turned_ref, opposite_ref, out_ref):
    half = SHARDS // 2
    group = lax.broadcasted_iota(jnp.int32, (SHARDS, 128), 1) // REST
    rest = [[jnp.zeros((SHARDS, 128), F32) for _ in range(3)] for _ in range(2)]

    def put(pair, lanes, value):
        value = value.astype(BF16)
        for yh in range(2):
            out_ref[yh, pair, :, lanes] = value[yh * half : (yh + 1) * half]

    for r in range(RB):
        rows = slice(r * SHARDS, (r + 1) * SHARDS)
        block = dot(turned_ref[rows, :], own_ref[...]) + dot(opposite_ref[rows, :], came_ref[...])
        for pair in range(2):
            put(pair, slice(r * MAIN, (r + 1) * MAIN), block[:, pair * MAIN : (pair + 1) * MAIN])
            tail = block[:, 2 * MAIN + pair * 128 : 2 * MAIN + (pair + 1) * 128]
            rest[pair][r // 4] = jnp.where(group == r % 4, tail, rest[pair][r // 4])
    for pair in range(2):
        for t in range(3):
            put(pair, slice(SPLIT + t * 128, SPLIT + (t + 1) * 128), rest[pair][t])


def block_kernel(place_ref, came_ref, block_ref, square_ref):
    rows = jnp.sum(came_ref[...].astype(F32), axis=0)
    sums = jnp.sum(rows * rows, axis=0, keepdims=True)
    square = functools.reduce(jnp.add, [sums[:, t * 128 : (t + 1) * 128] for t in range(WIDTH // 128)])
    square_ref[...] = jnp.broadcast_to(square[None], square_ref.shape)
    mine = lax.broadcasted_iota(jnp.int32, rows.shape, 0) == place_ref[6]
    own = jnp.sum(jnp.where(mine, rows, 0.0), axis=0, keepdims=True)
    for r in range(RB):
        block_ref[r : r + 1, :MAIN] = own[:, r * MAIN : (r + 1) * MAIN]
        block_ref[r : r + 1, MAIN:] = own[:, SPLIT + r * REST : SPLIT + (r + 1) * REST]


def clip_kernel(square_ref, block_ref, out_ref):
    square = jnp.sum(jnp.sum(square_ref[...], axis=0), keepdims=True)
    factor = jnp.minimum(1.0, math.sqrt(D * E) * lax.rsqrt(square))
    out_ref[...] = block_ref[...] * factor


def call(kernel, inputs, outputs, flops, size, name, spaces=(), scratch=()):
    specs = [SMEM if value.ndim == 1 else VMEM for value in inputs]
    for i in spaces:
        specs[i] = pl.BlockSpec(memory_space=pl.ANY)
    return pl.pallas_call(
        kernel,
        out_shape=[jax.ShapeDtypeStruct(shape, dtype) for shape, dtype in outputs],
        in_specs=specs,
        out_specs=[VMEM] * len(outputs),
        scratch_shapes=list(scratch),
        compiler_params=pltpu.CompilerParams(vmem_limit_bytes=size << 20),
        cost_estimate=pl.CostEstimate(flops=flops, bytes_accessed=4 << 20, transcendentals=0),
        name=name,
    )(*inputs)


def traded(value, axis):
    return lax.all_to_all(value, axis, split_axis=0, concat_axis=0)


def total(value):
    return jnp.sum(value.astype(F32), axis=0)


def local(image_embeds, text_features, projection, pair_step, pair_col):
    x = lax.axis_index("x")
    places = (RIGHT_AT, RIGHT2_AT, LEFT2_AT, ACROSS_AT)
    place = [lax.axis_index(DP)] + [position_of(x, at) for at in places]
    place = jnp.stack(place + [lax.axis_index("c"), lax.axis_index(("zh", "z1"))]).astype(jnp.int32)
    image = image_embeds[0]
    features = text_features[0]
    right = shifted(image, RIGHT)
    left = shifted(image, LEFT)
    right2 = shifted(right, RIGHT2)
    left2 = shifted(left, LEFT2)
    across = shifted(right, ACROSS)

    full = (ROWS, E)
    table = (8, ROWS)
    unit, inverse, texts, acc, steps, cols = call(
        first_kernel,
        (place, features, projection, image, pair_step, pair_col),
        ((full, F32), ((ROWS, 128), F32), (full, BF16), (full, F32), (table, jnp.int32), (table, jnp.int32)),
        1 << 30, 48, "hidden_and_own", range(1, 6),
        (
            pltpu.VMEM((ROWS, D), BF16), pltpu.VMEM((D, E), BF16), pltpu.VMEM(full, BF16),
            pltpu.VMEM(pair_step.shape, jnp.int32), pltpu.VMEM(pair_col.shape, jnp.int32), pltpu.SemaphoreType.DMA((5,)),
        ),
    )
    turned, pick_there, pick_here = call(
        order_kernel, (place, features), (((D, ROWS), BF16), ((E, PICK), BF16), ((E, PICK), BF16)), 1 << 30, 32, "order"
    )
    swap = [(0, 1), (1, 0)]
    opposite = lax.ppermute(turned, "c", swap)
    (acc,) = call(near_kernel, (place, right, left, steps, cols, texts, acc), ((full, F32),), 1 << 30, 24, "near_pairs")
    for at, block, name in ((4, across, "far_across"), (2, right2, "far_right")):
        (acc,) = call(
            functools.partial(far_kernel, at), (place, block, steps, cols, texts, acc), ((full, F32),), 1 << 28, 24, name
        )
    grad, columns = call(
        last_kernel,
        (place, left2, steps, cols, texts, acc, unit, inverse, pick_there),
        ((full, BF16), ((ROWS, PICK), BF16)),
        1 << 30, 32, "far_left",
    )
    columns = lax.ppermute(columns, "c", swap)
    (own,) = call(own_kernel, (grad, pick_here), (((ROWS, PICK), BF16),), 1 << 28, 24, "own_columns")
    (both,) = call(
        partial_kernel, (own, columns, turned, opposite), (((2, 2, SHARDS // 2, WIDTH), BF16),), 1 << 30, 32, "partial"
    )
    rows = total(traded(both.reshape(32, 8, WIDTH), NEAR)).astype(BF16)
    near = lax.ppermute(rows, "z1", swap)
    (grad_text,) = call(text_kernel, (grad, projection), ((full, BF16),), 1 << 28, 24, "grad_text")
    near, grad_text = lax.optimization_barrier((near, grad_text))
    rows = (rows.astype(F32) + near.astype(F32)).astype(BF16)
    rows = traded(jnp.broadcast_to(rows[None], (4, 8, WIDTH)), "zh")
    block, square = call(block_kernel, (place, rows), (((RB, CB), F32), ((64, 1, 128), F32)), 1 << 20, 16, "block")
    square = traded(square, NEAR + ("c",))
    (block,) = call(clip_kernel, (square, block), (((RB, CB), F32),), 1 << 20, 16, "clip")
    return (grad_text[None], block)


def solution(mesh):
    split = Mesh(mesh.devices.reshape(SHAPE), AXES)
    placed = (
        P(OUTER, DP, None),
        P(OUTER, DP, None),
        P(),
        P(OUTER, None),
        P(OUTER, None),
    )
    return jax.shard_map(
        local,
        mesh=split,
        in_specs=placed,
        out_specs=(P(OUTER, DP, None), P(DP, OUTER)),
        check_vma=False,
    )
```

```python
import functools
import math

import jax
import jax.numpy as jnp
from jax import lax
from jax.experimental import pallas as pl
from jax.experimental.pallas import tpu as pltpu
from jax.sharding import Mesh, PartitionSpec as P

LOGIT_SCALE = 10.0
LOGIT_BIAS = -3.0
LOSS_SCALE = 256.0
EPSILON = 1e-06

SHARDS = 128
ROWS = 256
D = 1152
E = 1152
SHAPE = (2, 4, 2, 2, 4, 2, 2)
AXES = ("yh", "zh", "z1", "z0", "x", "yl", "c")
DP = ("yh", "zh", "z1", "z0", "x")
OUTER = ("yl", "c")
NEAR = ("yh", "yl", "x", "z0")
RB = 9
CB = 288
MAIN = 256
REST = 32
SPLIT = RB * MAIN
WIDTH = 2688
PICK = 2 * MAIN + 2 * 128

F32 = jnp.float32
BF16 = jnp.bfloat16
VMEM = pl.BlockSpec(memory_space=pltpu.VMEM)
SMEM = pl.BlockSpec(memory_space=pltpu.SMEM)


RIGHT = (1, 1, 1, -3)
LEFT = (-1, -1, -1, -1)
RIGHT2 = (1, 1, 1, 1)
LEFT2 = (-1, -1, 3, -1)
ACROSS = (4, -4, -4, -4)
RIGHT_AT = (5, 1, 1, 1)
LEFT_AT = (3, 3, 3, 3)
RIGHT2_AT = (0, 4, 0, 0)
LEFT2_AT = (4, 0, 4, 4)
ACROSS_AT = (1, 5, 5, 5)


def shifted(value, hops):
    pairs = [(source, (source + hops[source % 4]) % SHARDS) for source in range(SHARDS)]
    return lax.ppermute(value, DP, pairs)


def position_of(x, places):
    return jnp.where(x == 0, places[0], jnp.where(x == 1, places[1], jnp.where(x == 2, places[2], places[3])))


def dot(a, b):
    return jnp.dot(a, b, preferred_element_type=F32)


def dot_t(a, b):
    return lax.dot_general(a, b, (((1,), (1,)), ((), ())), preferred_element_type=F32)


def unit_rows(values):
    values = values.astype(F32)
    inverse = lax.rsqrt(jnp.sum(values * values, axis=-1, keepdims=True) + EPSILON)
    return values * inverse, inverse


def pair_grad(step_ref, col_ref, texts, block, position):
    images = unit_rows(block)[0].astype(BF16)
    steps = step_ref[pl.ds(position, 1), :]
    cols = col_ref[pl.ds(position, 1), :]
    logits = LOGIT_SCALE * dot_t(texts, images) + LOGIT_BIAS
    rows = lax.broadcasted_iota(jnp.int32, logits.shape, 0)
    positive = (steps == position) & (cols == rows)
    scale = LOSS_SCALE * LOGIT_SCALE
    chance = 1.0 / (1.0 + jnp.exp(jnp.where(positive, logits, -logits)))
    weights = (jnp.where(positive, -scale, scale) * chance).astype(BF16)
    return dot(weights, images)


def first_kernel(
    place_ref, feat_hbm, proj_hbm, image_hbm, step_hbm, col_hbm, unit_ref, inv_ref, text_ref, acc_ref, steps_ref, cols_ref,
    feat_ref, proj_ref, image_ref, step_ref, col_ref, sems,
):
    pairs = (
        (feat_hbm, feat_ref), (proj_hbm, proj_ref), (image_hbm, image_ref), (step_hbm, step_ref), (col_hbm, col_ref)
    )
    copies = [pltpu.make_async_copy(src, dst, sems.at[i]) for i, (src, dst) in enumerate(pairs)]
    for copy in copies:
        copy.start()
    copies[0].wait()
    copies[1].wait()
    hidden = dot(feat_ref[...], proj_ref[...])
    unit, inverse = unit_rows(hidden)
    texts = unit.astype(BF16)
    unit_ref[...] = unit
    inv_ref[...] = jnp.broadcast_to(inverse, inv_ref.shape)
    text_ref[...] = texts
    for copy in copies[2:]:
        copy.wait()
    for position in range(8):
        shard = (place_ref[0] + (position + (SHARDS - 2))) & (SHARDS - 1)
        spot = pl.ds(pl.multiple_of(shard * ROWS, ROWS), ROWS)
        steps_ref[position : position + 1, :] = step_ref[:, spot]
        cols_ref[position : position + 1, :] = col_ref[:, spot]
    acc_ref[...] = pair_grad(steps_ref, cols_ref, texts, image_ref[...], 2)


def near_kernel(place_ref, right_ref, left_ref, step_ref, col_ref, text_ref, acc_ref, out_ref):
    texts = text_ref[...]
    total = acc_ref[...] + pair_grad(step_ref, col_ref, texts, right_ref[...], place_ref[1])
    out_ref[...] = total + pair_grad(step_ref, col_ref, texts, left_ref[...], 3)


def column_of(lane, core):
    tail = lane - 2 * MAIN
    pair = jnp.where(lane < 2 * MAIN, lane >> 8, tail >> 7)
    inside = jnp.where(lane < 2 * MAIN, lane & (MAIN - 1), MAIN + (lane & (REST - 1)))
    return CB * (2 * pair + core) + inside


def order_kernel(place_ref, feat_ref, turned_ref, there_ref, here_ref):
    spot = lax.broadcasted_iota(jnp.int32, (D, 1), 0)
    within, peer = spot >> 7, spot & (SHARDS - 1)
    yh, x, z0, z = peer >> 6, (peer >> 4) & 3, (peer >> 3) & 1, peer & 7
    source = RB * (64 * yh + 8 * z + 4 * z0 + x) + within
    lanes = lax.broadcasted_iota(jnp.int32, (D, D), 1)
    order = jnp.where(lanes == source, 1.0, 0.0).astype(BF16)
    turned_ref[...] = dot_t(order, feat_ref[...]).astype(BF16)
    core = place_ref[5]
    lane = lax.broadcasted_iota(jnp.int32, (1, PICK), 1)
    rows = lax.broadcasted_iota(jnp.int32, (E, PICK), 0)
    there_ref[...] = jnp.where(rows == column_of(lane, 1 - core), 1.0, 0.0).astype(BF16)
    here_ref[...] = jnp.where(rows == column_of(lane, core), 1.0, 0.0).astype(BF16)


def far_kernel(at, place_ref, image_ref, step_ref, col_ref, text_ref, acc_ref, out_ref):
    part = pair_grad(step_ref, col_ref, text_ref[...], image_ref[...], place_ref[at])
    out_ref[...] = acc_ref[...] + part


def last_kernel(
    place_ref, left_ref, step_ref, col_ref, text_ref, acc_ref, unit_ref, inv_ref, pick_ref, grad_ref, out_ref
):
    part = pair_grad(step_ref, col_ref, text_ref[...], left_ref[...], place_ref[3])
    total = acc_ref[...] + part
    unit = unit_ref[...]
    radial = jnp.sum(unit * total, axis=-1, keepdims=True)
    grad = (inv_ref[:, :1] * (total - unit * radial)).astype(BF16)
    grad_ref[...] = grad
    out_ref[...] = dot(grad, pick_ref[...]).astype(BF16)


def own_kernel(grad_ref, pick_ref, out_ref):
    out_ref[...] = dot(grad_ref[...], pick_ref[...]).astype(BF16)


def text_kernel(grad_ref, proj_hbm, out_ref, proj_ref, sem):
    copy = pltpu.make_async_copy(proj_hbm, proj_ref, sem)
    copy.start()
    copy.wait()
    out_ref[...] = dot_t(grad_ref[...], proj_ref[...]).astype(BF16)


def partial_kernel(own_ref, came_ref, turned_ref, opposite_ref, out_ref):
    half = SHARDS // 2
    group = lax.broadcasted_iota(jnp.int32, (SHARDS, 128), 1) // REST
    rest = [[jnp.zeros((SHARDS, 128), F32) for _ in range(3)] for _ in range(2)]

    def put(pair, lanes, value):
        value = value.astype(BF16)
        for yh in range(2):
            out_ref[yh, pair, :, lanes] = value[yh * half : (yh + 1) * half]

    for r in range(RB):
        rows = slice(r * SHARDS, (r + 1) * SHARDS)
        block = dot(turned_ref[rows, :], own_ref[...]) + dot(opposite_ref[rows, :], came_ref[...])
        for pair in range(2):
            put(pair, slice(r * MAIN, (r + 1) * MAIN), block[:, pair * MAIN : (pair + 1) * MAIN])
            tail = block[:, 2 * MAIN + pair * 128 : 2 * MAIN + (pair + 1) * 128]
            rest[pair][r // 4] = jnp.where(group == r % 4, tail, rest[pair][r // 4])
    for pair in range(2):
        for t in range(3):
            put(pair, slice(SPLIT + t * 128, SPLIT + (t + 1) * 128), rest[pair][t])


def block_kernel(place_ref, came_ref, block_ref, square_ref):
    rows = jnp.sum(came_ref[...].astype(F32), axis=0)
    sums = jnp.sum(rows * rows, axis=0, keepdims=True)
    square = functools.reduce(jnp.add, [sums[:, t * 128 : (t + 1) * 128] for t in range(WIDTH // 128)])
    square_ref[...] = jnp.broadcast_to(square[None], square_ref.shape)
    mine = lax.broadcasted_iota(jnp.int32, rows.shape, 0) == place_ref[6]
    own = jnp.sum(jnp.where(mine, rows, 0.0), axis=0, keepdims=True)
    for r in range(RB):
        block_ref[r : r + 1, :MAIN] = own[:, r * MAIN : (r + 1) * MAIN]
        block_ref[r : r + 1, MAIN:] = own[:, SPLIT + r * REST : SPLIT + (r + 1) * REST]


def clip_kernel(square_ref, block_ref, out_ref):
    square = jnp.sum(jnp.sum(square_ref[...], axis=0), keepdims=True)
    factor = jnp.minimum(1.0, math.sqrt(D * E) * lax.rsqrt(square))
    out_ref[...] = block_ref[...] * factor


def call(kernel, inputs, outputs, flops, size, name, spaces=(), scratch=()):
    specs = [SMEM if value.ndim == 1 else VMEM for value in inputs]
    for i in spaces:
        specs[i] = pl.BlockSpec(memory_space=pl.ANY)
    return pl.pallas_call(
        kernel,
        out_shape=[jax.ShapeDtypeStruct(shape, dtype) for shape, dtype in outputs],
        in_specs=specs,
        out_specs=[VMEM] * len(outputs),
        scratch_shapes=list(scratch),
        compiler_params=pltpu.CompilerParams(vmem_limit_bytes=size << 20),
        cost_estimate=pl.CostEstimate(flops=flops, bytes_accessed=4 << 20, transcendentals=0),
        name=name,
    )(*inputs)


def traded(value, axis):
    return lax.all_to_all(value, axis, split_axis=0, concat_axis=0)


def total(value):
    return jnp.sum(value.astype(F32), axis=0)


def local(image_embeds, text_features, projection, pair_step, pair_col):
    x = lax.axis_index("x")
    places = (RIGHT_AT, RIGHT2_AT, LEFT2_AT, ACROSS_AT)
    place = [lax.axis_index(DP)] + [position_of(x, at) for at in places]
    place = jnp.stack(place + [lax.axis_index("c"), lax.axis_index(("zh", "z1"))]).astype(jnp.int32)
    image = image_embeds[0]
    features = text_features[0]
    right = shifted(image, RIGHT)
    left = shifted(image, LEFT)
    right2 = shifted(right, RIGHT2)
    left2 = shifted(left, LEFT2)
    across = shifted(right, ACROSS)

    full = (ROWS, E)
    table = (8, ROWS)
    unit, inverse, texts, acc, steps, cols = call(
        first_kernel,
        (place, features, projection, image, pair_step, pair_col),
        ((full, F32), ((ROWS, 128), F32), (full, BF16), (full, F32), (table, jnp.int32), (table, jnp.int32)),
        1 << 30, 48, "hidden_and_own", range(1, 6),
        (
            pltpu.VMEM((ROWS, D), BF16), pltpu.VMEM((D, E), BF16), pltpu.VMEM(full, BF16),
            pltpu.VMEM(pair_step.shape, jnp.int32), pltpu.VMEM(pair_col.shape, jnp.int32), pltpu.SemaphoreType.DMA((5,)),
        ),
    )
    turned, pick_there, pick_here = call(
        order_kernel, (place, features), (((D, ROWS), BF16), ((E, PICK), BF16), ((E, PICK), BF16)), 1 << 30, 32, "order"
    )
    swap = [(0, 1), (1, 0)]
    opposite = lax.ppermute(turned, "c", swap)
    (acc,) = call(near_kernel, (place, right, left, steps, cols, texts, acc), ((full, F32),), 1 << 30, 24, "near_pairs")
    for at, block, name in ((4, across, "far_across"), (2, right2, "far_right")):
        (acc,) = call(
            functools.partial(far_kernel, at), (place, block, steps, cols, texts, acc), ((full, F32),), 1 << 28, 24, name
        )
    grad, columns = call(
        last_kernel,
        (place, left2, steps, cols, texts, acc, unit, inverse, pick_there),
        ((full, BF16), ((ROWS, PICK), BF16)),
        1 << 30, 32, "far_left",
    )
    columns = lax.ppermute(columns, "c", swap)
    (own,) = call(own_kernel, (grad, pick_here), (((ROWS, PICK), BF16),), 1 << 28, 24, "own_columns")
    (both,) = call(
        partial_kernel, (own, columns, turned, opposite), (((2, 2, SHARDS // 2, WIDTH), BF16),), 1 << 30, 32, "partial"
    )
    rows = total(traded(both.reshape(32, 8, WIDTH), NEAR)).astype(BF16)
    near = lax.ppermute(rows, "z1", swap)
    (grad_text,) = call(
        text_kernel, (grad, projection), ((full, BF16),), 1 << 28, 52, "grad_text", (1,),
        (pltpu.VMEM((D, E), BF16), pltpu.SemaphoreType.DMA),
    )
    near, grad_text = lax.optimization_barrier((near, grad_text))
    rows = (rows.astype(F32) + near.astype(F32)).astype(BF16)
    rows = traded(jnp.broadcast_to(rows[None], (4, 8, WIDTH)), "zh")
    block, square = call(block_kernel, (place, rows), (((RB, CB), F32), ((64, 1, 128), F32)), 1 << 20, 16, "block")
    square = traded(square, NEAR + ("c",))
    (block,) = call(clip_kernel, (square, block), (((RB, CB), F32),), 1 << 20, 16, "clip")
    return (grad_text[None], block)


def solution(mesh):
    split = Mesh(mesh.devices.reshape(SHAPE), AXES)
    placed = (
        P(OUTER, DP, None),
        P(OUTER, DP, None),
        P(),
        P(OUTER, None),
        P(OUTER, None),
    )
    return jax.shard_map(
        local,
        mesh=split,
        in_specs=placed,
        out_specs=(P(OUTER, DP, None), P(DP, OUTER)),
        check_vma=False,
    )
```

```python
import functools
import math

import jax
import jax.numpy as jnp
from jax import lax
from jax.experimental import pallas as pl
from jax.experimental.pallas import tpu as pltpu
from jax.sharding import Mesh, PartitionSpec as P

LOGIT_SCALE = 10.0
LOGIT_BIAS = -3.0
LOSS_SCALE = 256.0
EPSILON = 1e-06

SHARDS = 128
ROWS = 256
D = 1152
E = 1152
SHAPE = (2, 4, 2, 2, 4, 2, 2)
AXES = ("yh", "zh", "z1", "z0", "x", "yl", "c")
DP = ("yh", "zh", "z1", "z0", "x")
OUTER = ("yl", "c")
NEAR = ("yh", "yl", "x", "z0")
RB = 9
CB = 288
MAIN = 256
REST = 32
SPLIT = RB * MAIN
WIDTH = 2688
STRIP = 16
PICK = 2 * MAIN + 2 * 128

F32 = jnp.float32
BF16 = jnp.bfloat16
VMEM = pl.BlockSpec(memory_space=pltpu.VMEM)
SMEM = pl.BlockSpec(memory_space=pltpu.SMEM)


RIGHT = (1, 1, 1, -3)
LEFT = (-1, -1, -1, -1)
RIGHT2 = (1, 1, 1, 1)
LEFT2 = (-1, -1, 3, -1)
ACROSS = (4, -4, -4, -4)
RIGHT_AT = (5, 1, 1, 1)
LEFT_AT = (3, 3, 3, 3)
RIGHT2_AT = (0, 4, 0, 0)
LEFT2_AT = (4, 0, 4, 4)
ACROSS_AT = (1, 5, 5, 5)


def shifted(value, hops):
    pairs = [(source, (source + hops[source % 4]) % SHARDS) for source in range(SHARDS)]
    return lax.ppermute(value, DP, pairs)


def position_of(x, places):
    return jnp.where(x == 0, places[0], jnp.where(x == 1, places[1], jnp.where(x == 2, places[2], places[3])))


def dot(a, b):
    return jnp.dot(a, b, preferred_element_type=F32)


def dot_t(a, b):
    return lax.dot_general(a, b, (((1,), (1,)), ((), ())), preferred_element_type=F32)


def unit_rows(values):
    values = values.astype(F32)
    inverse = lax.rsqrt(jnp.sum(values * values, axis=-1, keepdims=True) + EPSILON)
    return values * inverse, inverse


def pair_grad(step_ref, col_ref, texts, block_ref, image_ref, position):
    for row in range(0, ROWS, STRIP):
        image_ref[row : row + STRIP, :] = unit_rows(block_ref[row : row + STRIP, :])[0].astype(BF16)
    images = image_ref[...]
    steps = step_ref[pl.ds(position, 1), :]
    cols = col_ref[pl.ds(position, 1), :]
    logits = LOGIT_SCALE * dot_t(texts, images) + LOGIT_BIAS
    rows = lax.broadcasted_iota(jnp.int32, logits.shape, 0)
    positive = (steps == position) & (cols == rows)
    scale = LOSS_SCALE * LOGIT_SCALE
    chance = 1.0 / (1.0 + jnp.exp(jnp.where(positive, logits, -logits)))
    weights = (jnp.where(positive, -scale, scale) * chance).astype(BF16)
    return dot(weights, images)


def first_kernel(
    place_ref, feat_hbm, proj_hbm, image_hbm, step_hbm, col_hbm, unit_ref, inv_ref, text_ref, acc_ref, steps_ref, cols_ref,
    feat_ref, proj_ref, image_ref, step_ref, col_ref, sems,
):
    pairs = (
        (feat_hbm, feat_ref), (proj_hbm, proj_ref), (image_hbm, image_ref), (step_hbm, step_ref), (col_hbm, col_ref)
    )
    copies = [pltpu.make_async_copy(src, dst, sems.at[i]) for i, (src, dst) in enumerate(pairs)]
    for copy in copies:
        copy.start()
    copies[0].wait()
    copies[1].wait()
    hidden = dot(feat_ref[...], proj_ref[...])
    unit, inverse = unit_rows(hidden)
    texts = unit.astype(BF16)
    unit_ref[...] = unit
    inv_ref[...] = jnp.broadcast_to(inverse, inv_ref.shape)
    text_ref[...] = texts
    for copy in copies[2:]:
        copy.wait()
    for position in range(8):
        shard = (place_ref[0] + (position + (SHARDS - 2))) & (SHARDS - 1)
        spot = pl.ds(pl.multiple_of(shard * ROWS, ROWS), ROWS)
        steps_ref[position : position + 1, :] = step_ref[:, spot]
        cols_ref[position : position + 1, :] = col_ref[:, spot]
    acc_ref[...] = pair_grad(steps_ref, cols_ref, texts, image_ref, image_ref, 2)


def near_kernel(place_ref, right_ref, left_ref, step_ref, col_ref, text_ref, acc_ref, out_ref, *scratch):
    texts = text_ref[...]
    total = acc_ref[...] + pair_grad(step_ref, col_ref, texts, right_ref, scratch[0], place_ref[1])
    out_ref[...] = total + pair_grad(step_ref, col_ref, texts, left_ref, scratch[1], 3)


def column_of(lane, core):
    tail = lane - 2 * MAIN
    pair = jnp.where(lane < 2 * MAIN, lane >> 8, tail >> 7)
    inside = jnp.where(lane < 2 * MAIN, lane & (MAIN - 1), MAIN + (lane & (REST - 1)))
    return CB * (2 * pair + core) + inside


def order_kernel(place_ref, feat_ref, turned_ref, there_ref, here_ref):
    spot = lax.broadcasted_iota(jnp.int32, (D, 1), 0)
    within, peer = spot >> 7, spot & (SHARDS - 1)
    yh, x, z0, z = peer >> 6, (peer >> 4) & 3, (peer >> 3) & 1, peer & 7
    source = RB * (64 * yh + 8 * z + 4 * z0 + x) + within
    lanes = lax.broadcasted_iota(jnp.int32, (D, D), 1)
    order = jnp.where(lanes == source, 1.0, 0.0).astype(BF16)
    turned_ref[...] = dot_t(order, feat_ref[...]).astype(BF16)
    core = place_ref[5]
    lane = lax.broadcasted_iota(jnp.int32, (1, PICK), 1)
    rows = lax.broadcasted_iota(jnp.int32, (E, PICK), 0)
    there_ref[...] = jnp.where(rows == column_of(lane, 1 - core), 1.0, 0.0).astype(BF16)
    here_ref[...] = jnp.where(rows == column_of(lane, core), 1.0, 0.0).astype(BF16)


def far_kernel(at, place_ref, image_ref, step_ref, col_ref, text_ref, acc_ref, out_ref, scratch):
    part = pair_grad(step_ref, col_ref, text_ref[...], image_ref, scratch, place_ref[at])
    out_ref[...] = acc_ref[...] + part


def last_kernel(
    place_ref, left_ref, step_ref, col_ref, text_ref, acc_ref, unit_ref, inv_ref, pick_ref, grad_ref, out_ref, scratch
):
    part = pair_grad(step_ref, col_ref, text_ref[...], left_ref, scratch, place_ref[3])
    for row in range(0, ROWS, STRIP):
        strip = slice(row, row + STRIP)
        total = acc_ref[strip, :] + part[strip]
        unit = unit_ref[strip, :]
        radial = jnp.sum(unit * total, axis=-1, keepdims=True)
        grad_ref[strip, :] = (inv_ref[strip, :1] * (total - unit * radial)).astype(BF16)
    out_ref[...] = dot(grad_ref[...], pick_ref[...]).astype(BF16)


def own_kernel(grad_ref, pick_ref, proj_ref, out_ref, text_ref):
    out_ref[...] = dot(grad_ref[...], pick_ref[...]).astype(BF16)
    text_ref[...] = dot_t(grad_ref[...], proj_ref[...]).astype(BF16)


def partial_kernel(own_ref, came_ref, turned_ref, opposite_ref, out_ref):
    half = SHARDS // 2
    group = lax.broadcasted_iota(jnp.int32, (SHARDS, 128), 1) // REST
    rest = [[jnp.zeros((SHARDS, 128), F32) for _ in range(3)] for _ in range(2)]

    def put(pair, lanes, value):
        value = value.astype(BF16)
        for yh in range(2):
            out_ref[yh, pair, :, lanes] = value[yh * half : (yh + 1) * half]

    for r in range(RB):
        rows = slice(r * SHARDS, (r + 1) * SHARDS)
        block = dot(turned_ref[rows, :], own_ref[...]) + dot(opposite_ref[rows, :], came_ref[...])
        for pair in range(2):
            put(pair, slice(r * MAIN, (r + 1) * MAIN), block[:, pair * MAIN : (pair + 1) * MAIN])
            tail = block[:, 2 * MAIN + pair * 128 : 2 * MAIN + (pair + 1) * 128]
            rest[pair][r // 4] = jnp.where(group == r % 4, tail, rest[pair][r // 4])
    for pair in range(2):
        for t in range(3):
            put(pair, slice(SPLIT + t * 128, SPLIT + (t + 1) * 128), rest[pair][t])


def block_kernel(place_ref, came_ref, block_ref, square_ref):
    rows = jnp.sum(came_ref[...].astype(F32), axis=0)
    sums = jnp.sum(rows * rows, axis=0, keepdims=True)
    square = functools.reduce(jnp.add, [sums[:, t * 128 : (t + 1) * 128] for t in range(WIDTH // 128)])
    square_ref[...] = jnp.broadcast_to(square[None], square_ref.shape)
    mine = lax.broadcasted_iota(jnp.int32, rows.shape, 0) == place_ref[6]
    own = jnp.sum(jnp.where(mine, rows, 0.0), axis=0, keepdims=True)
    for r in range(RB):
        block_ref[r : r + 1, :MAIN] = own[:, r * MAIN : (r + 1) * MAIN]
        block_ref[r : r + 1, MAIN:] = own[:, SPLIT + r * REST : SPLIT + (r + 1) * REST]


def clip_kernel(square_ref, block_ref, out_ref):
    square = jnp.sum(jnp.sum(square_ref[...], axis=0), keepdims=True)
    factor = jnp.minimum(1.0, math.sqrt(D * E) * lax.rsqrt(square))
    out_ref[...] = block_ref[...] * factor


def call(kernel, inputs, outputs, flops, size, name, spaces=(), scratch=()):
    specs = [SMEM if value.ndim == 1 else VMEM for value in inputs]
    for i in spaces:
        specs[i] = pl.BlockSpec(memory_space=pl.ANY)
    return pl.pallas_call(
        kernel,
        out_shape=[jax.ShapeDtypeStruct(shape, dtype) for shape, dtype in outputs],
        in_specs=specs,
        out_specs=[VMEM] * len(outputs),
        scratch_shapes=list(scratch),
        compiler_params=pltpu.CompilerParams(vmem_limit_bytes=size << 20),
        cost_estimate=pl.CostEstimate(flops=flops, bytes_accessed=4 << 20, transcendentals=0),
        name=name,
    )(*inputs)


def traded(value, axis):
    return lax.all_to_all(value, axis, split_axis=0, concat_axis=0)


def total(value):
    return jnp.sum(value.astype(F32), axis=0)


def local(image_embeds, text_features, projection, pair_step, pair_col):
    x = lax.axis_index("x")
    places = (RIGHT_AT, RIGHT2_AT, LEFT2_AT, ACROSS_AT)
    place = [lax.axis_index(DP)] + [position_of(x, at) for at in places]
    place = jnp.stack(place + [lax.axis_index("c"), lax.axis_index(("zh", "z1"))]).astype(jnp.int32)
    image = image_embeds[0]
    features = text_features[0]
    right = shifted(image, RIGHT)
    left = shifted(image, LEFT)
    right2 = shifted(right, RIGHT2)
    left2 = shifted(left, LEFT2)
    across = shifted(right, ACROSS)

    full = (ROWS, E)
    table = (8, ROWS)
    strips = (pltpu.VMEM(full, BF16),)
    unit, inverse, texts, acc, steps, cols = call(
        first_kernel,
        (place, features, projection, image, pair_step, pair_col),
        ((full, F32), ((ROWS, 128), F32), (full, BF16), (full, F32), (table, jnp.int32), (table, jnp.int32)),
        1 << 30, 48, "hidden_and_own", range(1, 6),
        (
            pltpu.VMEM((ROWS, D), BF16), pltpu.VMEM((D, E), BF16), pltpu.VMEM(full, BF16),
            pltpu.VMEM(pair_step.shape, jnp.int32), pltpu.VMEM(pair_col.shape, jnp.int32), pltpu.SemaphoreType.DMA((5,)),
        ),
    )
    turned, pick_there, pick_here = call(
        order_kernel, (place, features), (((D, ROWS), BF16), ((E, PICK), BF16), ((E, PICK), BF16)), 1 << 30, 32, "order"
    )
    swap = [(0, 1), (1, 0)]
    opposite = lax.ppermute(turned, "c", swap)
    (acc,) = call(near_kernel, (place, right, left, steps, cols, texts, acc), ((full, F32),), 1 << 30, 24, "near_pairs", (), strips * 2)
    for at, block, name in ((4, across, "far_across"), (2, right2, "far_right")):
        (acc,) = call(
            functools.partial(far_kernel, at), (place, block, steps, cols, texts, acc), ((full, F32),), 1 << 28, 24, name, (), strips
        )
    grad, columns = call(
        last_kernel,
        (place, left2, steps, cols, texts, acc, unit, inverse, pick_there),
        ((full, BF16), ((ROWS, PICK), BF16)),
        1 << 30, 32, "far_left", (), strips,
    )
    columns = lax.ppermute(columns, "c", swap)
    own, grad_text = call(
        own_kernel, (grad, pick_here, projection), (((ROWS, PICK), BF16), (full, BF16)), 1 << 28, 24, "own_columns"
    )
    (both,) = call(
        partial_kernel, (own, columns, turned, opposite), (((2, 2, SHARDS // 2, WIDTH), BF16),), 1 << 30, 32, "partial"
    )
    rows = total(traded(both.reshape(32, 8, WIDTH), NEAR)).astype(BF16)
    near = lax.ppermute(rows, "z1", swap)
    rows = (rows.astype(F32) + near.astype(F32)).astype(BF16)
    rows = traded(jnp.broadcast_to(rows[None], (4, 8, WIDTH)), "zh")
    block, square = call(block_kernel, (place, rows), (((RB, CB), F32), ((64, 1, 128), F32)), 1 << 20, 16, "block")
    square = traded(square, NEAR + ("c",))
    (block,) = call(clip_kernel, (square, block), (((RB, CB), F32),), 1 << 20, 16, "clip")
    return (grad_text[None], block)


def solution(mesh):
    split = Mesh(mesh.devices.reshape(SHAPE), AXES)
    placed = (
        P(OUTER, DP, None),
        P(OUTER, DP, None),
        P(),
        P(OUTER, None),
        P(OUTER, None),
    )
    return jax.shard_map(
        local,
        mesh=split,
        in_specs=placed,
        out_specs=(P(OUTER, DP, None), P(DP, OUTER)),
        check_vma=False,
    )
```
